256 devices in a mesh: grp: 16 (over z, core), dev: 16 (over y, x).
Axes of the slice: x: 4, y: 4, z: 8, core: 2. Of those that a mesh axis runs over, the one named last changes fastest.
Arguments:
- features: bfloat16 [3072, 512, 128], P(('grp', 'dev')), may hold values from -6 to 6
- occupancy: int32 [3072, 512], P(('grp', 'dev')), may hold values 0 or 1
- w_first: bfloat16 [27, 128, 128], replicated, may hold values from -0.125 to 0.125
- w_second: bfloat16 [27, 128, 128], replicated, may hold values from -0.125 to 0.125
- src_ref: int32 [3072, 27], P(('grp', 'dev')), may hold values from -1 to 31, as said below
- send_list: int32 [256, 16, 1], P(('grp', 'dev')), may hold values from -1 to 11, as said below
Outputs:
- block_out: bfloat16 [3072, 512, 128], P(('grp', 'dev'))
The draws below stay inside these ranges and needn't reach their ends.
Inputs may be any that keep to these rules, and one draw needn't show every extreme that they name: Entry src_ref[b, 13] is b's own position among its device's bricks. Entries 0 to 11 are the device's own bricks, the next 2 the lower end set, the next 2 the upper one, then one slot for each device p of the coarse range in order of p. No entry refers to an end set that does not exist or to a slot whose send_list entry is -1; every slot that carries a brick is referred to by some entry of the receiving device. `send_list`: A device sends nothing to itself; in every coarse range, each device receives one brick from the device just after it in its range, counted cyclically.
All inputs are finite; a program needn't handle non-finite values. No bound on the sum of `occupancy` on one device may be relied on, other than what follows from the above.
Results may differ from the reference program's by a relative error of at most 0.0031.
Values may be sent and summed in bfloat16 or wider, within the bound.
No kernel may reach another device: no remote copies, remote signals or barrier semaphores. Data moves between devices by JAX's collectives and lax.ppermute only.
A program may use at most 128 MiB of HBM per device.

```python
import jax
import jax.numpy as jnp
from jax import lax

C = 128
VOX = 512
BR = 12
EDGE = 2
CAP = 1
BRICKS = 3072
N_GRP = 16
N_DEV = 16
DEVICES = 256


def receive_counts(key):
    inner_key = jax.random.fold_in(key, 11)
    counts = jax.random.randint(inner_key, (DEVICES, N_DEV), 0, CAP + 1)
    ranks = jnp.arange(DEVICES)
    inner = ranks % N_DEV
    column = jnp.arange(N_DEV)[None, :]
    counts = jnp.where(column == ((inner + 1) % N_DEV)[:, None], CAP, counts)
    counts = jnp.where(column == inner[:, None], 0, counts)
    return counts.astype(jnp.int32)


def draw_send_list(key, part):
    counts = receive_counts(key)
    key = jax.random.fold_in(key, 3)
    senders = jnp.arange(DEVICES)
    receivers = (senders // N_DEV)[:, None] * N_DEV + jnp.arange(N_DEV)[None, :]
    number = counts[receivers, (senders % N_DEV)[:, None]]
    values = jax.random.randint(key, (DEVICES, N_DEV, CAP), 0, BR)
    slots = jnp.arange(CAP)[None, None, :]
    return jnp.where(slots < number[:, :, None], values, -1).astype(jnp.int32)


def draw_src_ref(key, part):
    counts = receive_counts(key)
    key = jax.random.fold_in(key, 5)
    pool_size = BR + 2 * EDGE + N_DEV * CAP
    ranks = jnp.arange(DEVICES)
    own_ok = jnp.ones((DEVICES, BR), jnp.int32)
    lower_ok = jnp.broadcast_to((ranks > 0)[:, None], (DEVICES, EDGE)).astype(jnp.int32)
    upper_ok = jnp.broadcast_to((ranks < DEVICES - 1)[:, None], (DEVICES, EDGE)).astype(jnp.int32)
    slot_ok = (jnp.arange(CAP)[None, None, :] < counts[:, :, None]).astype(jnp.int32).reshape(DEVICES, N_DEV * CAP)
    usable = jnp.concatenate([own_ok, lower_ok, upper_ok, slot_ok], axis=1)
    places = 26 * BR
    keys = jax.random.split(jax.random.fold_in(key, 1), DEVICES)
    order = jax.vmap(lambda k: jax.random.permutation(k, places))(keys)
    first_pick = jnp.minimum(order, pool_size - 1)
    first_ok = (order < pool_size) & (jnp.take_along_axis(usable, first_pick, axis=1) > 0)
    guess = jax.random.randint(jax.random.fold_in(key, 2), (DEVICES, places), 0, pool_size)
    guess_ok = jnp.take_along_axis(usable, guess, axis=1) > 0
    fallback = jax.random.randint(jax.random.fold_in(key, 3), (DEVICES, places), 0, BR)
    absent = jax.random.randint(jax.random.fold_in(key, 4), (DEVICES, places), 0, 3) == 0
    other = jnp.where(absent, -1, jnp.where(guess_ok, guess, fallback))
    chosen = jnp.where(first_ok, order, other).reshape(DEVICES, BR, 26)
    centre = jnp.broadcast_to(jnp.arange(BR)[None, :, None], (DEVICES, BR, 1))
    full = jnp.concatenate([chosen[:, :, :13], centre, chosen[:, :, 13:]], axis=2)
    return full.reshape(DEVICES * BR, 27).astype(jnp.int32)


def set_ends(array, key, smallest, largest):
    index_at = [jax.random.randint(jax.random.fold_in(key, axis), (), 0, length) for axis, length in enumerate(array.shape)]
    widest = array.shape.index(max(array.shape))
    beside = index_at[:widest] + [(index_at[widest] + 1) % array.shape[widest]] + index_at[widest + 1:]
    return array.at[tuple(index_at)].set(smallest).at[tuple(beside)].set(largest)


def levels(key, dims, cuts, smallest, largest):
    def one(dim, shards_of):
        heights = jax.random.uniform(jax.random.fold_in(jax.random.fold_in(key, 6), dim), (shards_of,), jnp.float32, smallest / len(cuts), largest / len(cuts))
        return jnp.repeat(jnp.exp(heights), dims[dim] // shards_of).reshape((-1,) + (1,) * (len(dims) - dim - 1))

    gain = one(*cuts[0])
    for cut in cuts[1:]:
        gain = gain * one(*cut)
    return gain


def scatter_about(key, dims, width, bound, pieces=(), kind=jnp.bfloat16):
    result = jax.random.normal(key, dims, jnp.float32) * width
    if len(pieces) > 0:
        result = levels(key, dims, pieces, -0.22, 0.18) * result
    return jnp.clip(result, min=-bound, max=bound).astype(kind)


def setup_inputs(seed: int = 0) -> dict:
    splits = jax.random.split(jax.random.key(seed), 7)
    features = scatter_about(splits[0], (BRICKS, VOX, C), 1.0, 6.0, ((0, 256),))
    occupancy = set_ends((jax.random.randint(splits[1], (BRICKS, VOX), 0, 2) < 1).astype(jnp.int32), jax.random.fold_in(splits[1], 1), 0, 1)
    w_first = scatter_about(splits[2], (27, C, C), (14 * C) ** -0.5, 0.125)
    w_second = scatter_about(splits[3], (27, C, C), (14 * C) ** -0.5, 0.125)
    src_ref = draw_src_ref(jax.random.fold_in(splits[6], 71), 0)
    send_list = draw_send_list(jax.random.fold_in(splits[6], 71), 0)
    return dict(features=features, occupancy=occupancy, w_first=w_first, w_second=w_second, src_ref=src_ref, send_list=send_list)


def slab_bounds(delta):
    if delta < 0:
        return 7, 8
    if delta == 0:
        return 0, 8
    return 0, 1


def assemble(source, refs):
    planes = []
    for dx in (-1, 0, 1):
        rows = []
        for dy in (-1, 0, 1):
            cols = []
            for dz in (-1, 0, 1):
                index = (dx + 1) * 9 + (dy + 1) * 3 + (dz + 1)
                a0, a1 = slab_bounds(dx)
                b0, b1 = slab_bounds(dy)
                c0, c1 = slab_bounds(dz)
                part = source[:, a0:a1, b0:b1, c0:c1]
                cols.append(jnp.take(part, refs[:, index], axis=0))
            rows.append(jnp.concatenate(cols, axis=3))
        planes.append(jnp.concatenate(rows, axis=2))
    return jnp.concatenate(planes, axis=1)


def convolve(padded, weights):
    chans = padded.shape[-1]
    wide = weights.reshape(9, 3 * chans, chans)
    total = jnp.zeros((padded.shape[0] * 512, chans), jnp.float32)
    for ax in range(3):
        for ay in range(3):
            stacked = jnp.concatenate([padded[:, ax:ax + 8, ay:ay + 8, az:az + 8] for az in range(3)], axis=-1)
            total = total + jnp.dot(stacked.reshape(-1, 3 * chans), wide[ax * 3 + ay], preferred_element_type=jnp.float32)
    return total.reshape(padded.shape[0], 512, chans)


def reference(features, occupancy, w_first, w_second, src_ref, send_list):
    count = N_GRP * N_DEV
    ranks = jnp.arange(count).astype(jnp.int32)
    own = ranks[:, None] * BR + jnp.arange(BR).astype(jnp.int32)[None, :]
    edge_ids = jnp.arange(EDGE).astype(jnp.int32)[None, :]
    lower = jnp.where(ranks[:, None] > 0, (ranks[:, None] - 1) * BR + BR - EDGE + edge_ids, BRICKS)
    upper = jnp.where(ranks[:, None] < count - 1, (ranks[:, None] + 1) * BR + edge_ids, BRICKS)
    group = ranks // N_DEV
    inner = ranks % N_DEV
    senders = group[:, None] * N_DEV + jnp.arange(N_DEV).astype(jnp.int32)[None, :]
    picks = send_list[senders, inner[:, None]]
    remote = jnp.where(picks >= 0, senders[:, :, None] * BR + picks, BRICKS).reshape(count, -1)
    blank = jnp.full((count, 1), BRICKS, jnp.int32)
    table = jnp.concatenate([own, lower, upper, remote, blank], axis=1).astype(jnp.int32)
    pool_size = BR + 2 * EDGE + N_DEV * CAP
    local_refs = jnp.where(src_ref < 0, pool_size, src_ref).astype(jnp.int32).reshape(count, BR * 27)
    global_refs = jnp.take_along_axis(table, local_refs, axis=1).reshape(count, BR, 27)
    chans = features.shape[-1]
    held = occupancy.astype(jnp.bfloat16)
    x = features * held[:, :, None]
    zero_brick = jnp.zeros((1, 8, 8, 8, chans), jnp.bfloat16)
    source = jnp.concatenate([x.reshape(BRICKS, 8, 8, 8, chans), zero_brick], axis=0)
    mask_dev = occupancy.astype(jnp.float32).reshape(count, BR, 512)

    def first(args):
        refs, mask = args
        acc = convolve(assemble(source, refs), w_first)
        return (jax.nn.silu(acc) * mask[:, :, None]).astype(jnp.bfloat16)

    hidden = lax.map(first, (global_refs, mask_dev)).reshape(BRICKS, 512, chans)
    source_two = jnp.concatenate([hidden.reshape(BRICKS, 8, 8, 8, chans), zero_brick], axis=0)
    x_dev = x.reshape(count, BR, 512, chans)

    def second(args):
        refs, mask, own_x = args
        acc = convolve(assemble(source_two, refs), w_second)
        return ((own_x.astype(jnp.float32) + acc) * mask[:, :, None]).astype(jnp.bfloat16)

    return lax.map(second, (global_refs, mask_dev, x_dev)).reshape(BRICKS, 512, chans)
```

```python
import functools

import jax
import jax.numpy as jnp
from jax import lax
from jax.experimental import pallas as pl
from jax.experimental.pallas import tpu as pltpu
from jax.sharding import PartitionSpec as P

BR = 12
EDGE = 2
SLOTS = 16
ENTRIES = BR + 2 * EDGE + SLOTS
BLANK = ENTRIES
SHELL = 304
FACE_LO = 224
FACE_HI = 260
VMEM_BYTES = 56 * 1024 * 1024


def ring_row(x, y):
    if x == 0:
        return y * 8
    if x == 7:
        return 64 + y * 8
    if y == 0:
        return 128 + (x - 1) * 8
    if y == 7:
        return 176 + (x - 1) * 8
    return None


def cell_row(x, y, z):
    first = ring_row(x, y)
    if first is not None:
        return first + z
    return (FACE_LO if z == 0 else FACE_HI) + (x - 1) * 6 + (y - 1)


def write_shell(cells, packed):
    packed[0:64, :] = cells[0:64, :]
    packed[64:128, :] = cells[448:512, :]
    for x in range(1, 7):
        packed[128 + (x - 1) * 8 : 136 + (x - 1) * 8, :] = cells[x * 64 : x * 64 + 8, :]
        packed[176 + (x - 1) * 8 : 184 + (x - 1) * 8, :] = cells[x * 64 + 56 : x * 64 + 64, :]
        packed[FACE_LO + (x - 1) * 6 : FACE_LO + x * 6, :] = cells[pl.ds(x * 64 + 8, 6, stride=8), :]
        packed[FACE_HI + (x - 1) * 6 : FACE_HI + x * 6, :] = cells[pl.ds(x * 64 + 15, 6, stride=8), :]
    packed[296:304, :] = jnp.zeros((8, 128), jnp.float32)


def pack_kernel(send_ref, feat_ref, mask_ref, shells_ref, out_ref, low_ref, high_ref, cells, packed):
    step = pl.program_id(0)
    for half in range(2):
        brick = step * 2 + half
        cells[...] = feat_ref[half].astype(jnp.float32) * mask_ref[half].astype(jnp.float32)
        write_shell(cells, packed)
        shells_ref[brick] = packed[...].astype(jnp.bfloat16)

    @pl.when(step == BR // 2 - 1)
    def _():
        low_ref[...] = shells_ref[BR - EDGE :]
        high_ref[...] = shells_ref[:EDGE]
        for slot in range(SLOTS):
            out_ref[slot] = shells_ref[jnp.maximum(send_ref[slot], 0)]


def pack(send, feats, masks):
    whole = lambda *dims: pl.BlockSpec(dims, lambda i: (0,) * len(dims))
    shape = lambda n: jax.ShapeDtypeStruct((n, SHELL, 128), jnp.bfloat16)
    return pl.pallas_call(
        pack_kernel,
        grid=(BR // 2,),
        in_specs=[
            pl.BlockSpec(memory_space=pltpu.SMEM),
            pl.BlockSpec((2, 512, 128), lambda i: (i, 0, 0)),
            pl.BlockSpec((2, 512, 128), lambda i: (i, 0, 0)),
        ],
        out_specs=[whole(BR, SHELL, 128), whole(SLOTS, SHELL, 128), whole(EDGE, SHELL, 128), whole(EDGE, SHELL, 128)],
        out_shape=[shape(BR), shape(SLOTS), shape(EDGE), shape(EDGE)],
        scratch_shapes=[pltpu.VMEM((512, 128), jnp.float32), pltpu.VMEM((SHELL, 128), jnp.float32)],
        compiler_params=pltpu.CompilerParams(vmem_limit_bytes=VMEM_BYTES),
        name="pack_shells",
    )(send, feats, masks)


def build_weights(w_ref, wide):
    zero = jnp.zeros((128, 128), jnp.bfloat16)
    for tap in range(9):
        w0, w1, w2 = w_ref[tap], w_ref[9 + tap], w_ref[18 + tap]
        wide[tap, 0, 0:128, 0:128] = w0
        wide[tap, 0, 0:128, 128:256] = zero
        wide[tap, 0, 128:256, 0:128] = w1
        wide[tap, 0, 128:256, 128:256] = w0
        wide[tap, 1, 0:128, 0:128] = w2
        wide[tap, 1, 0:128, 128:256] = w1
        wide[tap, 1, 128:256, 0:128] = zero
        wide[tap, 1, 128:256, 128:256] = w2


def build_pool(pool, shells_ref, before_ref, after_ref, recv_ref):
    for entry in range(BR):
        pool[entry] = shells_ref[entry].astype(jnp.float32)
    for entry in range(EDGE):
        pool[BR + entry] = before_ref[entry].astype(jnp.float32)
        pool[BR + EDGE + entry] = after_ref[entry].astype(jnp.float32)
    for entry in range(SLOTS):
        pool[BR + 2 * EDGE + entry] = recv_ref[entry].astype(jnp.float32)
    pool[BLANK] = jnp.zeros((SHELL, 128), jnp.float32)


def build_block(step, src_ref, own_rows, pool, block):
    sub = lax.broadcasted_iota(jnp.int32, (8, 128), 0)
    first, last = sub == 0, sub == 7
    entries = []
    for half in range(2):
        refs = [src_ref[step * 2 + half, k] for k in range(27)]
        entries.append([jnp.where(r < 0, BLANK, r) for r in refs])
    for px in range(10):
        dx = 0 if px == 0 else (2 if px == 9 else 1)
        x = 7 if px == 0 else (0 if px == 9 else px - 1)
        rows = [own_rows(half, x) for half in range(2)] if dx == 1 else None
        for py in range(10):
            dy = 0 if py == 0 else (2 if py == 9 else 1)
            y = 7 if py == 0 else (0 if py == 9 else py - 1)
            base = dx * 9 + dy * 3
            parts = []
            for half in range(2):
                here, below, above = entries[half][base + 1], entries[half][base], entries[half][base + 2]
                if dx == 1 and dy == 1:
                    mid = rows[half][y * 8 : y * 8 + 8]
                else:
                    at = ring_row(x, y)
                    mid = pool[here, at : at + 8, :]
                at_lo, at_hi = cell_row(x, y, 7), cell_row(x, y, 0)
                lo = jnp.broadcast_to(pool[below, at_lo : at_lo + 1, :], (8, 128))
                hi = jnp.broadcast_to(pool[above, at_hi : at_hi + 1, :], (8, 128))
                parts.append(
                    (
                        jnp.where(first, lo, pltpu.roll(mid, 1, 0)),
                        mid,
                        jnp.where(last, hi, pltpu.roll(mid, 7, 0)),
                    )
                )
            lanes = slice((px % 2) * 128, (px % 2) * 128 + 128)
            for az in range(3):
                both = jnp.concatenate([parts[0][az], parts[1][az]], axis=0)
                block[az, px // 2, py, :, lanes] = both.astype(jnp.bfloat16)


def multiply(block, wide):
    acc = jnp.zeros((512, 256), jnp.float32)
    for az in range(3):
        for ay in range(3):
            for side in range(2):
                part = block[az, side : side + 4, ay : ay + 8].reshape(512, 256)
                acc = acc + jnp.dot(part, wide[ay * 3 + az, side], preferred_element_type=jnp.float32)
    return acc.reshape(4, 8, 16, 256)


def take(acc, half, x):
    lanes = (x % 2) * 128
    return acc[x // 2, :, half * 8 : half * 8 + 8, lanes : lanes + 128].reshape(64, 128)


def first_kernel(
    src_ref, send_ref, feat_ref, mask_ref, shells_ref, before_ref, after_ref, recv_ref, w_ref,
    hidden_ref, own_ref, out_ref, low_ref, high_ref,
    pool, wide, block, cells, packed,
):
    step = pl.program_id(0)

    @pl.when(step == 0)
    def _():
        build_weights(w_ref, wide)
        build_pool(pool, shells_ref, before_ref, after_ref, recv_ref)

    def own_rows(half, x):
        rows = pl.ds(x * 64, 64)
        return feat_ref[half, rows, :].astype(jnp.float32) * mask_ref[half, rows, :].astype(jnp.float32)

    build_block(step, src_ref, own_rows, pool, block)
    acc = multiply(block, wide)
    for half in range(2):
        for x in range(8):
            rows = slice(x * 64, x * 64 + 64)
            v = take(acc, half, x)
            value = v / (1.0 + jnp.exp(-v)) * mask_ref[half, rows, :].astype(jnp.float32)
            cells[rows, :] = value
            hidden_ref[half, rows, :] = value.astype(jnp.bfloat16)
        write_shell(cells, packed)
        own_ref[step * 2 + half] = packed[...].astype(jnp.bfloat16)

    @pl.when(step == BR // 2 - 1)
    def _():
        low_ref[...] = own_ref[BR - EDGE :]
        high_ref[...] = own_ref[:EDGE]
        for slot in range(SLOTS):
            out_ref[slot] = own_ref[jnp.maximum(send_ref[slot], 0)]


def second_kernel(
    src_ref, feat_ref, mask_ref, hidden_ref, shells_ref, before_ref, after_ref, recv_ref, w_ref,
    result_ref,
    pool, wide, block,
):
    step = pl.program_id(0)

    @pl.when(step == 0)
    def _():
        build_weights(w_ref, wide)
        build_pool(pool, shells_ref, before_ref, after_ref, recv_ref)

    def own_rows(half, x):
        return hidden_ref[half, pl.ds(x * 64, 64), :].astype(jnp.float32)

    build_block(step, src_ref, own_rows, pool, block)
    acc = multiply(block, wide)
    for half in range(2):
        for x in range(8):
            rows = slice(x * 64, x * 64 + 64)
            mask = mask_ref[half, rows, :].astype(jnp.float32)
            own = feat_ref[half, rows, :].astype(jnp.float32) * mask
            result_ref[half, rows, :] = ((own + take(acc, half, x)) * mask).astype(jnp.bfloat16)


WHOLE = functools.partial(pl.BlockSpec, memory_space=pltpu.VMEM)
SCALARS = functools.partial(pl.BlockSpec, memory_space=pltpu.SMEM)


def pair_spec():
    return pl.BlockSpec((2, 512, 128), lambda i: (i, 0, 0))


def conv_scratch():
    return [
        pltpu.VMEM((ENTRIES + 1, SHELL, 128), jnp.float32),
        pltpu.VMEM((9, 2, 256, 256), jnp.bfloat16),
        pltpu.VMEM((3, 5, 10, 16, 256), jnp.bfloat16),
    ]


def cost(extra):
    return pl.CostEstimate(flops=2 * 6 * 512 * 4608 * 256, bytes_accessed=8 << 20, transcendentals=extra)


def first(src, send, feats, masks, shells, before, after, recv, weights):
    whole = lambda n: pl.BlockSpec((n, SHELL, 128), lambda i: (0, 0, 0))
    shape = lambda n: jax.ShapeDtypeStruct((n, SHELL, 128), jnp.bfloat16)
    return pl.pallas_call(
        first_kernel,
        grid=(BR // 2,),
        in_specs=[SCALARS(), SCALARS(), pair_spec(), pair_spec()] + [WHOLE()] * 5,
        out_specs=[pair_spec(), whole(BR), whole(SLOTS), whole(EDGE), whole(EDGE)],
        out_shape=[jax.ShapeDtypeStruct((BR, 512, 128), jnp.bfloat16), shape(BR), shape(SLOTS), shape(EDGE), shape(EDGE)],
        scratch_shapes=conv_scratch() + [pltpu.VMEM((512, 128), jnp.float32), pltpu.VMEM((SHELL, 128), jnp.float32)],
        compiler_params=pltpu.CompilerParams(vmem_limit_bytes=VMEM_BYTES),
        cost_estimate=cost(BR * 512 * 128),
        name="first_conv",
    )(src, send, feats, masks, shells, before, after, recv, weights)


def second(src, feats, masks, hidden, shells, before, after, recv, weights):
    return pl.pallas_call(
        second_kernel,
        grid=(BR // 2,),
        in_specs=[SCALARS(), pair_spec(), pair_spec(), pair_spec()] + [WHOLE()] * 5,
        out_specs=pair_spec(),
        out_shape=jax.ShapeDtypeStruct((BR, 512, 128), jnp.bfloat16),
        scratch_shapes=conv_scratch(),
        compiler_params=pltpu.CompilerParams(vmem_limit_bytes=VMEM_BYTES),
        cost_estimate=cost(0),
        name="second_conv",
    )(src, feats, masks, hidden, shells, before, after, recv, weights)


def shifted(value, axis, steps):
    count = lax.axis_size(axis)
    initial, last = (max(0, -steps), min(count, count - steps))
    return lax.ppermute(value, axis, [(source, source + steps) for source in range(initial, last)])


def exchange(outgoing, low, high):
    arrived = lax.all_to_all(outgoing, "dev", split_axis=0, concat_axis=0, tiled=True)
    before = shifted(low, ("grp", "dev"), 1)
    after = shifted(high, ("grp", "dev"), -1)
    return before, after, arrived


def per_device(features, occupancy, w_first, w_second, src_ref, send_list):
    send = send_list.reshape(SLOTS)
    masks = jnp.broadcast_to(occupancy.astype(jnp.bfloat16)[:, :, None], features.shape)
    shells, outgoing, low, high = pack(send, features, masks)
    before, after, arrived = exchange(outgoing, low, high)
    hidden, shells, outgoing, low, high = first(
        src_ref, send, features, masks, shells, before, after, arrived, w_first
    )
    before, after, arrived = exchange(outgoing, low, high)
    return second(src_ref, features, masks, hidden, shells, before, after, arrived, w_second)


def solution(mesh):
    placed = (
        P(("grp", "dev"), None, None),
        P(("grp", "dev"), None),
        P(),
        P(),
        P(("grp", "dev"), None),
        P(("grp", "dev"), None, None),
    )
    return jax.shard_map(
        per_device,
        mesh=mesh,
        in_specs=placed,
        out_specs=P(("grp", "dev"), None, None),
        check_vma=False,
    )
```

```python
import functools

import jax
import jax.numpy as jnp
import numpy as np
from jax import lax
from jax.experimental import pallas as pl
from jax.experimental.pallas import tpu as pltpu
from jax.sharding import PartitionSpec as P

BR = 12
EDGE = 2
SLOTS = 16
ENTRIES = BR + 2 * EDGE + SLOTS
BLANK = ENTRIES
SHELL = 304
FACE_LO = 224
FACE_HI = 260
MIB = 1024 * 1024
LIMIT = 62


def ring_row(x, y):
    if x == 0:
        return y * 8
    if x == 7:
        return 64 + y * 8
    if y == 0:
        return 128 + (x - 1) * 8
    if y == 7:
        return 176 + (x - 1) * 8
    return None


def cell_row(x, y, z):
    first = ring_row(x, y)
    if first is not None:
        return first + z
    return (FACE_LO if z == 0 else FACE_HI) + (x - 1) * 6 + (y - 1)


def shell_matrix():
    picked = np.zeros((SHELL, 512), np.float32)
    for x in range(8):
        for y in range(8):
            for z in range(8):
                cell = x * 64 + y * 8 + z
                first = ring_row(x, y)
                if first is not None:
                    picked[first + z, cell] = 1
                elif z in (0, 7):
                    picked[cell_row(x, y, z), cell] = 1
    return jnp.asarray(picked, jnp.bfloat16)


def start_all(copies):
    for copy in copies:
        copy.start()
    return copies


def wait_all(copies):
    for copy in copies:
        copy.wait()


def hand_out(send_ref, own, out_ref, low_ref, high_ref, sems):
    copies = [pltpu.make_async_copy(own.at[:EDGE], high_ref, sems.at[SLOTS])]
    copies.append(pltpu.make_async_copy(own.at[BR - EDGE :], low_ref, sems.at[SLOTS + 1]))
    for slot in range(SLOTS):
        brick = jnp.maximum(send_ref[slot], 0)
        copies.append(pltpu.make_async_copy(own.at[brick], out_ref.at[slot], sems.at[slot]))
    return start_all(copies)


def pack_kernel(
    send_ref, feat_ref, occ_ref, pick_ref, out_ref, low_ref, high_ref, feats, own, in_sems, out_sems
):
    pairs = [pl.ds(pair * 2, 2) for pair in range(BR // 2)]
    loads = start_all(
        [pltpu.make_async_copy(feat_ref.at[at], feats.at[at], in_sems.at[n]) for n, at in enumerate(pairs)]
    )
    for pair, load in enumerate(loads):
        load.wait()
        for brick in (2 * pair, 2 * pair + 1):
            held = occ_ref[brick : brick + 1, :].astype(jnp.float32).astype(jnp.bfloat16)
            chooser = pick_ref[...] * jnp.broadcast_to(held, (SHELL, 512))
            shell = jnp.dot(chooser, feats[brick], preferred_element_type=jnp.float32)
            own[brick] = shell.astype(jnp.bfloat16)
    wait_all(hand_out(send_ref, own, out_ref, low_ref, high_ref, out_sems))


def toeplitz(target, taps):
    t0, t1, t2 = taps
    zero = jnp.zeros((128, 128), jnp.bfloat16)
    target[0, 0:128, 0:128] = t0
    target[0, 0:128, 128:256] = zero
    target[0, 128:256, 0:128] = t1
    target[0, 128:256, 128:256] = t0
    target[1, 0:128, 0:128] = t2
    target[1, 0:128, 128:256] = t1
    target[1, 128:256, 0:128] = zero
    target[1, 128:256, 128:256] = t2


def edge_masks():
    sub = lax.broadcasted_iota(jnp.int32, (8, 128), 0)
    return sub == 0, sub == 7


def shift_down(value, first, fill):
    return jnp.where(first, fill, pltpu.roll(value, 1, 0))


def shift_up(value, last, fill):
    return jnp.where(last, fill, pltpu.roll(value, 7, 0))


def own_conv(plane, w_ref, part_ref, wide, block, base=None):
    step = pl.program_id(0)

    @pl.when(step == 0)
    def _():
        block[...] = jnp.zeros_like(block)
        for tap in range(9):
            toeplitz(wide.at[tap], (w_ref[tap], w_ref[9 + tap], w_ref[18 + tap]))

    first, last = edge_masks()
    for x in range(8):
        planes = [plane(half, x) for half in range(2)]
        px = x + 1
        lanes = slice((px % 2) * 128, (px % 2) * 128 + 128)
        for y in range(8):
            mids = [planes[half][y * 8 : y * 8 + 8] for half in range(2)]
            for az, parts in enumerate(
                (
                    [shift_down(mid, first, 0.0) for mid in mids],
                    mids,
                    [shift_up(mid, last, 0.0) for mid in mids],
                )
            ):
                block[az, px // 2, y + 1, :, lanes] = jnp.concatenate(parts, axis=0).astype(jnp.bfloat16)
    acc = jnp.zeros((512, 256), jnp.float32)
    for az in range(3):
        for ay in range(3):
            for side in range(2):
                part = block[az, side : side + 4, ay : ay + 8].reshape(512, 256)
                acc = acc + jnp.dot(part, wide[ay * 3 + az, side], preferred_element_type=jnp.float32)
    if base is None:
        part_ref[0] = acc
        return
    for half in range(2):
        for x in range(8):
            added = base(half, x)
            lanes = slice((x % 2) * 128, (x % 2) * 128 + 128)
            for y in range(8):
                row = (x // 2) * 128 + y * 16 + half * 8
                part_ref[0, row : row + 8, lanes] = acc[row : row + 8, lanes] + added[y * 8 : y * 8 + 8]


def first_own_kernel(feat_ref, occ_ref, pick_ref, w_ref, part_ref, x_ref, mask_ref, shell_ref, wide, block):
    step = pl.program_id(0)
    rows = lax.broadcasted_iota(jnp.int32, (128, 128), 0)
    cols = lax.broadcasted_iota(jnp.int32, (128, 128), 1)
    diagonal = rows == cols
    ones = jnp.ones((128, 128), jnp.bfloat16)
    held = {}
    for half in range(2):
        occupied = occ_ref[pl.ds(step * 2 + half, 1), :].astype(jnp.float32)
        for chunk in range(4):
            cells = slice(chunk * 128, chunk * 128 + 128)
            scale = jnp.where(diagonal, jnp.broadcast_to(occupied[:, cells], (128, 128)), 0.0).astype(jnp.bfloat16)
            right = jnp.concatenate([feat_ref[half, cells, :], ones], axis=1)
            both = jnp.dot(scale, right, preferred_element_type=jnp.float32)
            x_ref[half, cells, :] = both[:, :128].astype(jnp.bfloat16)
            mask_ref[half, cells, :] = both[:, 128:].astype(jnp.bfloat16)
            held[half, 2 * chunk] = both[:64, :128]
            held[half, 2 * chunk + 1] = both[64:, :128]
        shell = jnp.dot(pick_ref[...], x_ref[half], preferred_element_type=jnp.float32)
        shell_ref[half] = shell.astype(jnp.bfloat16)
    own_conv(lambda half, x: held[half, x], w_ref, part_ref, wide, block)


def second_own_kernel(hidden_ref, x_ref, pick_ref, w_ref, part_ref, shell_ref, wide, block):
    for half in range(2):
        shell = jnp.dot(pick_ref[...], hidden_ref[half], preferred_element_type=jnp.float32)
        shell_ref[half] = shell.astype(jnp.bfloat16)
    plane = lambda ref: lambda half, x: ref[half, x * 64 : x * 64 + 64, :].astype(jnp.float32)
    own_conv(plane(hidden_ref), w_ref, part_ref, wide, block, plane(x_ref))


def fill_pool(pool, start, source):
    for entry in range(source.shape[0]):
        pool[start + entry] = source[entry].astype(jnp.float32)


def build_halos(pair, src_ref, pool, halo):
    first, last = edge_masks()
    entries = []
    for half in range(2):
        refs = [src_ref[pair * 2 + half, k] for k in range(27)]
        entries.append([jnp.where(r < 0, BLANK, r) for r in refs])
    at = pl.ds(pl.multiple_of(pair * 16, 16), 16)

    def put(face, outer, parts):
        lanes = slice((outer % 2) * 128, (outer % 2) * 128 + 128)
        for shift in range(3):
            both = jnp.concatenate([parts[0][shift], parts[1][shift]], axis=0)
            halo[face, shift, outer // 2, at, lanes] = both.astype(jnp.bfloat16)

    def column(half, base, x, y):
        below, here, above = (entries[half][base + dz] for dz in range(3))
        start, at_lo, at_hi = ring_row(x, y), cell_row(x, y, 7), cell_row(x, y, 0)
        mid = pool[here, start : start + 8, :]
        lo = jnp.broadcast_to(pool[below, at_lo : at_lo + 1, :], (8, 128))
        hi = jnp.broadcast_to(pool[above, at_hi : at_hi + 1, :], (8, 128))
        return shift_down(mid, first, lo), mid, shift_up(mid, last, hi)

    for face, (delta, cell, z_cell) in enumerate(((0, 7, 7), (2, 0, 0))):
        for outer in range(10):
            dy = 0 if outer == 0 else (2 if outer == 9 else 1)
            y = 7 if outer == 0 else (0 if outer == 9 else outer - 1)
            put(face, outer, [column(half, delta * 9 + dy * 3, cell, y) for half in range(2)])
        for x in range(8):
            put(2 + face, x + 1, [column(half, 9 + delta * 3, x, cell) for half in range(2)])
        for x in range(8):
            parts = []
            for half in range(2):
                entry = entries[half][12 + delta]
                if x in (0, 7):
                    mid = pool[entry, pl.ds(ring_row(x, 0) + z_cell, 8, stride=8), :]
                else:
                    start = cell_row(x, 1, z_cell) - 1
                    at_lo, at_hi = cell_row(x, 0, z_cell), cell_row(x, 7, z_cell)
                    mid = pool[entry, start : start + 8, :]
                    mid = jnp.where(first, jnp.broadcast_to(pool[entry, at_lo : at_lo + 1, :], (8, 128)), mid)
                    mid = jnp.where(last, jnp.broadcast_to(pool[entry, at_hi : at_hi + 1, :], (8, 128)), mid)
                parts.append((shift_down(mid, first, 0.0), mid, shift_up(mid, last, 0.0)))
            put(4 + face, x + 1, parts)


def halo_weights(w_ref, along):
    for face in range(2):
        end = 2 * face
        for shift in range(3):
            toeplitz(along.at[face, shift], [w_ref[end * 9 + tap * 3 + shift] for tap in range(3)])
            toeplitz(along.at[2 + face, shift], [w_ref[tap * 9 + end * 3 + shift] for tap in range(3)])
            toeplitz(along.at[4 + face, shift], [w_ref[tap * 9 + shift * 3 + end] for tap in range(3)])


def halo_sums(halo, along, sums):
    rows = 8 * BR
    for face in range(6):
        acc = jnp.zeros((4 * rows, 256), jnp.float32)
        for shift in range(3):
            for side in range(2):
                part = halo[face, shift, side : side + 4].reshape(4 * rows, 256)
                acc = acc + jnp.dot(part, along[face, shift, side], preferred_element_type=jnp.float32)
        sums[face] = acc.reshape(4, BR, 8, 256)


def halo_part(src_ref, sources, landed, sems, streams, stream_sems, pool, halo, along, sums):
    loads = start_all([pltpu.make_async_copy(a, b, sems.at[n]) for n, (a, b) in enumerate(zip(sources, landed))])
    for n, (source, target, size) in enumerate(streams):
        for pair in range(BR // 2):
            at = pl.ds(pair * size, size)
            pltpu.make_async_copy(source.at[at], target.at[at], stream_sems.at[n, pair]).start()
    pool[BLANK] = jnp.zeros((SHELL, 128), jnp.float32)
    for face in range(2, 6):
        for shift in range(3):
            halo[face, shift, 0, :, 0:128] = jnp.zeros((8 * BR, 128), jnp.bfloat16)
            halo[face, shift, 4, :, 128:256] = jnp.zeros((8 * BR, 128), jnp.bfloat16)
    loads[0].wait()
    halo_weights(landed[0], along)
    for load, start, field in zip(loads[1:], (0, BR, BR + EDGE, BR + 2 * EDGE), landed[1:]):
        load.wait()
        fill_pool(pool, start, field)

    def pair_body(pair, carry):
        build_halos(pair, src_ref, pool, halo)
        return carry

    lax.fori_loop(0, BR // 2, pair_body, 0)
    halo_sums(halo, along, sums)


def wait_stream(streams, stream_sems, pair):
    for n, (source, target, size) in enumerate(streams):
        at = pl.ds(pair * size, size)
        pltpu.make_async_copy(source.at[at], target.at[at], stream_sems.at[n, pair]).wait()


def whole_plane(part, sums, pair, half, x):
    first, last = edge_masks()
    brick = pair * 2 + half
    lanes = slice((x % 2) * 128, (x % 2) * 128 + 128)
    columns = []
    for y in range(8):
        row = (x // 2) * 128 + y * 16 + half * 8
        value = part[pair, row : row + 8, lanes]
        if x in (0, 7):
            value = value + sums[x // 7, y // 2, brick, :, (y % 2) * 128 : (y % 2) * 128 + 128]
        if y in (0, 7):
            value = value + sums[2 + y // 7, x // 2, brick, :, lanes]
        lo = jnp.broadcast_to(sums[4, x // 2, brick, y : y + 1, lanes], (8, 128))
        hi = jnp.broadcast_to(sums[5, x // 2, brick, y : y + 1, lanes], (8, 128))
        columns.append(value + jnp.where(first, lo, jnp.where(last, hi, 0.0)))
    return jnp.concatenate(columns, axis=0)


def first_halo_kernel(
    src_ref, send_ref, pick_ref, part_ref, mask_ref, w_ref, shells_ref, before_ref, after_ref, recv_ref,
    hidden_ref, out_ref, low_ref, high_ref,
    pool, halo, along, sums, w, shells, before, after, recv, part, mask, done, sems, stream_sems, done_sems,
    own, out_sems,
):
    streams = ((part_ref, part, 1), (mask_ref, mask, 2))
    sources = (w_ref, shells_ref, before_ref, after_ref, recv_ref)
    landed = (w, shells, before, after, recv)
    halo_part(src_ref, sources, landed, sems, streams, stream_sems, pool, halo, along, sums)

    def store(pair):
        at = pl.ds(pair * 2, 2)
        return pltpu.make_async_copy(done.at[at], hidden_ref.at[at], done_sems.at[pair])

    def pair_body(pair, carry):
        wait_stream(streams, stream_sems, pair)
        for half in range(2):
            brick = pair * 2 + half
            for x in range(8):
                rows = slice(x * 64, x * 64 + 64)
                value = whole_plane(part, sums, pair, half, x)
                value = value / (1.0 + jnp.exp(-value)) * mask[brick, rows, :].astype(jnp.float32)
                done[brick, rows, :] = value.astype(jnp.bfloat16)
            shell = jnp.dot(pick_ref[...], done[brick], preferred_element_type=jnp.float32)
            own[brick] = shell.astype(jnp.bfloat16)
        store(pair).start()
        return carry

    lax.fori_loop(0, BR // 2, pair_body, 0)
    copies = hand_out(send_ref, own, out_ref, low_ref, high_ref, out_sems)
    wait_all([store(pair) for pair in range(BR // 2)])
    wait_all(copies)


def second_halo_kernel(
    src_ref, part_ref, mask_ref, w_ref, shells_ref, before_ref, after_ref, recv_ref,
    result_ref,
    pool, halo, along, sums, w, shells, before, after, recv, part, mask, done, sems, stream_sems, done_sems,
):
    streams = ((part_ref, part, 1), (mask_ref, mask, 2))
    sources = (w_ref, shells_ref, before_ref, after_ref, recv_ref)
    landed = (w, shells, before, after, recv)
    halo_part(src_ref, sources, landed, sems, streams, stream_sems, pool, halo, along, sums)

    def store(pair):
        at = pl.ds(pair * 2, 2)
        return pltpu.make_async_copy(done.at[at], result_ref.at[at], done_sems.at[pair])

    def pair_body(pair, carry):
        wait_stream(streams, stream_sems, pair)
        for half in range(2):
            brick = pair * 2 + half
            for x in range(8):
                rows = slice(x * 64, x * 64 + 64)
                value = whole_plane(part, sums, pair, half, x)
                done[brick, rows, :] = (value * mask[brick, rows, :].astype(jnp.float32)).astype(jnp.bfloat16)
        store(pair).start()
        return carry

    lax.fori_loop(0, BR // 2, pair_body, 0)
    wait_all([store(pair) for pair in range(BR // 2)])


WHOLE = functools.partial(pl.BlockSpec, memory_space=pltpu.VMEM)
SCALARS = functools.partial(pl.BlockSpec, memory_space=pltpu.SMEM)
ANYWHERE = functools.partial(pl.BlockSpec, memory_space=pl.ANY)
GRID = (BR // 2,)
FIELD = jax.ShapeDtypeStruct((BR, 512, 128), jnp.bfloat16)
PARTIAL = jax.ShapeDtypeStruct((BR // 2, 512, 256), jnp.float32)


def pair_spec():
    return pl.BlockSpec((2, 512, 128), lambda i: (i, 0, 0))


def part_spec():
    return pl.BlockSpec((1, 512, 256), lambda i: (i, 0, 0))


def shell_pair_spec():
    return pl.BlockSpec((2, SHELL, 128), lambda i: (i, 0, 0))


def shells_of(*counts):
    return [jax.ShapeDtypeStruct((n, SHELL, 128), jnp.bfloat16) for n in counts]


def params(mib):
    return pltpu.CompilerParams(vmem_limit_bytes=mib * MIB)


def own_scratch():
    return [pltpu.VMEM((9, 2, 256, 256), jnp.bfloat16), pltpu.VMEM((3, 5, 10, 16, 256), jnp.bfloat16)]


def halo_scratch():
    shells = [pltpu.VMEM((n, SHELL, 128), jnp.bfloat16) for n in (BR, EDGE, EDGE, SLOTS)]
    return [
        pltpu.VMEM((ENTRIES + 1, SHELL, 128), jnp.float32),
        pltpu.VMEM((6, 3, 5, 8 * BR, 256), jnp.bfloat16),
        pltpu.VMEM((6, 3, 2, 256, 256), jnp.bfloat16),
        pltpu.VMEM((6, 4, BR, 8, 256), jnp.float32),
        pltpu.VMEM((27, 128, 128), jnp.bfloat16),
        *shells,
        pltpu.VMEM((BR // 2, 512, 256), jnp.float32),
        pltpu.VMEM((BR, 512, 128), jnp.bfloat16),
        pltpu.VMEM((BR, 512, 128), jnp.bfloat16),
        pltpu.SemaphoreType.DMA((5,)),
        pltpu.SemaphoreType.DMA((2, BR // 2)),
        pltpu.SemaphoreType.DMA((BR // 2,)),
    ]


def own_shells_scratch():
    return [pltpu.VMEM((BR, SHELL, 128), jnp.bfloat16), pltpu.SemaphoreType.DMA((SLOTS + 2,))]


OWN_COST = pl.CostEstimate(flops=2 * 6 * 512 * 4608 * 256, bytes_accessed=8 * MIB, transcendentals=0)
HALO_COST = pl.CostEstimate(flops=2 * 36 * 384 * 256 * 256, bytes_accessed=10 * MIB, transcendentals=0)


def pack(send, feats, occ, pick):
    return pl.pallas_call(
        pack_kernel,
        in_specs=[SCALARS(), ANYWHERE(), WHOLE(), WHOLE()],
        out_specs=[ANYWHERE()] * 3,
        out_shape=shells_of(SLOTS, EDGE, EDGE),
        scratch_shapes=[
            pltpu.VMEM((BR, 512, 128), jnp.bfloat16),
            pltpu.VMEM((BR, SHELL, 128), jnp.bfloat16),
            pltpu.SemaphoreType.DMA((BR // 2,)),
            pltpu.SemaphoreType.DMA((SLOTS + 2,)),
        ],
        compiler_params=params(LIMIT),
        name="pack_shells",
    )(send, feats, occ, pick)


def first_own(feats, occ, pick, weights):
    return pl.pallas_call(
        first_own_kernel,
        grid=GRID,
        in_specs=[pair_spec(), WHOLE(), WHOLE(), WHOLE()],
        out_specs=[part_spec(), pair_spec(), pair_spec(), shell_pair_spec()],
        out_shape=[PARTIAL, FIELD, FIELD] + shells_of(BR),
        scratch_shapes=own_scratch(),
        compiler_params=params(LIMIT),
        cost_estimate=OWN_COST,
        name="first_own",
    )(feats, occ, pick, weights)


def second_own(hidden, x, pick, weights):
    return pl.pallas_call(
        second_own_kernel,
        grid=GRID,
        in_specs=[pair_spec(), pair_spec(), WHOLE(), WHOLE()],
        out_specs=[part_spec(), shell_pair_spec()],
        out_shape=[PARTIAL] + shells_of(BR),
        scratch_shapes=own_scratch(),
        compiler_params=params(LIMIT),
        cost_estimate=OWN_COST,
        name="second_own",
    )(hidden, x, pick, weights)


def first_halo(src, send, pick, part, mask, weights, shells, before, after, recv):
    return pl.pallas_call(
        first_halo_kernel,
        in_specs=[SCALARS(), SCALARS(), WHOLE()] + [ANYWHERE()] * 7,
        out_specs=[ANYWHERE()] * 4,
        out_shape=[FIELD] + shells_of(SLOTS, EDGE, EDGE),
        scratch_shapes=halo_scratch() + own_shells_scratch(),
        compiler_params=params(LIMIT),
        cost_estimate=HALO_COST,
        name="first_halo",
    )(src, send, pick, part, mask, weights, shells, before, after, recv)


def second_halo(src, part, mask, weights, shells, before, after, recv):
    return pl.pallas_call(
        second_halo_kernel,
        in_specs=[SCALARS()] + [ANYWHERE()] * 7,
        out_specs=ANYWHERE(),
        out_shape=FIELD,
        scratch_shapes=halo_scratch(),
        compiler_params=params(LIMIT),
        cost_estimate=HALO_COST,
        name="second_halo",
    )(src, part, mask, weights, shells, before, after, recv)


def shifted(value, axis, steps):
    count = lax.axis_size(axis)
    initial, last = (max(0, -steps), min(count, count - steps))
    return lax.ppermute(value, axis, [(source, source + steps) for source in range(initial, last)])


def exchange(outgoing, low, high):
    arrived = lax.all_to_all(outgoing, "dev", split_axis=0, concat_axis=0, tiled=True)
    before = shifted(low, ("grp", "dev"), 1)
    after = shifted(high, ("grp", "dev"), -1)
    return before, after, arrived


def per_device(features, occupancy, w_first, w_second, src_ref, send_list):
    send = send_list.reshape(SLOTS)
    pick = shell_matrix()
    outgoing, low, high = pack(send, features, occupancy, pick)
    around = exchange(outgoing, low, high)
    part, x, mask, shells = first_own(features, occupancy, pick, w_first)
    hidden, outgoing, low, high = first_halo(src_ref, send, pick, part, mask, w_first, shells, *around)
    around = exchange(outgoing, low, high)
    part, shells = second_own(hidden, x, pick, w_second)
    return second_halo(src_ref, part, mask, w_second, shells, *around)


def solution(mesh):
    placed = (
        P(("grp", "dev"), None, None),
        P(("grp", "dev"), None),
        P(),
        P(),
        P(("grp", "dev"), None),
        P(("grp", "dev"), None, None),
    )
    return jax.shard_map(
        per_device,
        mesh=mesh,
        in_specs=placed,
        out_specs=P(("grp", "dev"), None, None),
        check_vma=False,
    )
```

```python
import functools

import jax
import jax.numpy as jnp
import numpy as np
from jax import lax
from jax.experimental import pallas as pl
from jax.experimental.pallas import tpu as pltpu
from jax.sharding import PartitionSpec as P

BR = 12
EDGE = 2
SLOTS = 16
ENTRIES = BR + 2 * EDGE + SLOTS
BLANK = ENTRIES
SHELL = 304
FACE_LO = 224
FACE_HI = 260
MIB = 1024 * 1024
VMEM_LIMIT = 64 * MIB - 96 * 1024


def ring_row(x, y):
    if x == 0:
        return y * 8
    if x == 7:
        return 64 + y * 8
    if y == 0:
        return 128 + (x - 1) * 8
    if y == 7:
        return 176 + (x - 1) * 8
    return None


def cell_row(x, y, z):
    first = ring_row(x, y)
    if first is not None:
        return first + z
    return (FACE_LO if z == 0 else FACE_HI) + (x - 1) * 6 + (y - 1)


def shell_matrix():
    picked = np.zeros((SHELL, 512), np.float32)
    for x in range(8):
        for y in range(8):
            for z in range(8):
                cell = x * 64 + y * 8 + z
                first = ring_row(x, y)
                if first is not None:
                    picked[first + z, cell] = 1
                elif z in (0, 7):
                    picked[cell_row(x, y, z), cell] = 1
    return jnp.asarray(picked, jnp.bfloat16)


def store_shell(shell, planes, cells=None, pick=None):
    shell[0:64, :] = planes[0].astype(jnp.bfloat16)
    shell[64:128, :] = planes[7].astype(jnp.bfloat16)
    for x in (1, 3, 5):
        for start, rows in ((128, slice(0, 8)), (176, slice(56, 64))):
            both = jnp.concatenate([planes[x][rows], planes[x + 1][rows]], axis=0)
            shell[start + (x - 1) * 8 : start + (x + 1) * 8, :] = both.astype(jnp.bfloat16)
    if cells is not None:
        inner = jnp.dot(pick, cells, preferred_element_type=jnp.float32)
        shell[FACE_LO:SHELL, :] = inner.astype(jnp.bfloat16)


def start_all(copies):
    for copy in copies:
        copy.start()
    return copies


def wait_all(copies):
    for copy in copies:
        copy.wait()


def hand_out(send_ref, own, out_ref, low_ref, high_ref, sems):
    copies = [pltpu.make_async_copy(own.at[:EDGE], high_ref, sems.at[SLOTS])]
    copies.append(pltpu.make_async_copy(own.at[BR - EDGE :], low_ref, sems.at[SLOTS + 1]))
    for slot in range(SLOTS):
        brick = jnp.maximum(send_ref[slot], 0)
        copies.append(pltpu.make_async_copy(own.at[brick], out_ref.at[slot], sems.at[slot]))
    return start_all(copies)


def pack_kernel(
    send_ref, feat_ref, occ_ref, pick_ref, out_ref, low_ref, high_ref, feats, own, pick, in_sems, out_sems
):
    pick_load = pltpu.make_async_copy(pick_ref, pick, in_sems.at[BR // 2])
    pick_load.start()
    pairs = [pl.ds(pair * 2, 2) for pair in range(BR // 2)]
    loads = start_all(
        [pltpu.make_async_copy(feat_ref.at[at], feats.at[at], in_sems.at[n]) for n, at in enumerate(pairs)]
    )
    pick_load.wait()
    for part in range(0, BR // 2, 3):
        wait_all(loads[part : part + 3])
        for brick in range(2 * part, 2 * part + 6):
            held = occ_ref[brick : brick + 1, :].astype(jnp.float32).astype(jnp.bfloat16)
            chooser = pick[...] * jnp.broadcast_to(held, (SHELL, 512))
            shell = jnp.dot(chooser, feats[brick], preferred_element_type=jnp.float32)
            own[brick] = shell.astype(jnp.bfloat16)
    wait_all(hand_out(send_ref, own, out_ref, low_ref, high_ref, out_sems))


def toeplitz(target, taps):
    t0, t1, t2 = taps
    zero = jnp.zeros((128, 128), jnp.bfloat16)
    target[0, 0:128, 0:128] = t0
    target[0, 0:128, 128:256] = zero
    target[0, 128:256, 0:128] = t1
    target[0, 128:256, 128:256] = t0
    target[1, 0:128, 0:128] = t2
    target[1, 0:128, 128:256] = t1
    target[1, 128:256, 0:128] = zero
    target[1, 128:256, 128:256] = t2


def edge_masks():
    sub = lax.broadcasted_iota(jnp.int32, (8, 128), 0)
    return sub == 0, sub == 7


def shift_down(value, first, fill):
    return jnp.where(first, fill, pltpu.roll(value, 1, 0))


def shift_up(value, last, fill):
    return jnp.where(last, fill, pltpu.roll(value, 7, 0))


def own_conv(plane, w_ref, part_ref, wide, block, base=None):
    step = pl.program_id(0)

    @pl.when(step == 0)
    def _():
        block[...] = jnp.zeros_like(block)
        for tap in range(9):
            toeplitz(wide.at[tap], (w_ref[tap], w_ref[9 + tap], w_ref[18 + tap]))

    first, last = edge_masks()
    for x in range(8):
        planes = [plane(half, x) for half in range(2)]
        px = x + 1
        lanes = slice((px % 2) * 128, (px % 2) * 128 + 128)
        for y in range(8):
            mids = [planes[half][y * 8 : y * 8 + 8] for half in range(2)]
            for az, parts in enumerate(
                (
                    [shift_down(mid, first, 0.0) for mid in mids],
                    mids,
                    [shift_up(mid, last, 0.0) for mid in mids],
                )
            ):
                block[az, px // 2, y + 1, :, lanes] = jnp.concatenate(parts, axis=0).astype(jnp.bfloat16)
    acc = jnp.zeros((512, 256), jnp.float32)
    for az in range(3):
        for ay in range(3):
            for side in range(2):
                part = block[az, side : side + 4, ay : ay + 8].reshape(512, 256)
                acc = acc + jnp.dot(part, wide[ay * 3 + az, side], preferred_element_type=jnp.float32)
    if base is None:
        part_ref[0] = acc
        return
    for half in range(2):
        for x in range(8):
            added = base(half, x)
            lanes = slice((x % 2) * 128, (x % 2) * 128 + 128)
            for y in range(8):
                row = (x // 2) * 128 + y * 16 + half * 8
                part_ref[0, row : row + 8, lanes] = acc[row : row + 8, lanes] + added[y * 8 : y * 8 + 8]


def first_own_kernel(feat_ref, occ_ref, pick_ref, w_ref, part_ref, x_ref, mask_ref, shell_ref, wide, block):
    step = pl.program_id(0)
    rows = lax.broadcasted_iota(jnp.int32, (128, 128), 0)
    cols = lax.broadcasted_iota(jnp.int32, (128, 128), 1)
    diagonal = rows == cols
    ones = jnp.ones((128, 128), jnp.bfloat16)
    held = {}
    for half in range(2):
        occupied = occ_ref[pl.ds(step * 2 + half, 1), :].astype(jnp.float32)
        for chunk in range(4):
            cells = slice(chunk * 128, chunk * 128 + 128)
            scale = jnp.where(diagonal, jnp.broadcast_to(occupied[:, cells], (128, 128)), 0.0).astype(jnp.bfloat16)
            right = jnp.concatenate([feat_ref[half, cells, :], ones], axis=1)
            both = jnp.dot(scale, right, preferred_element_type=jnp.float32)
            x_ref[half, cells, :] = both[:, :128].astype(jnp.bfloat16)
            mask_ref[half, cells, :] = both[:, 128:].astype(jnp.bfloat16)
            held[half, 2 * chunk] = both[:64, :128]
            held[half, 2 * chunk + 1] = both[64:, :128]
        store_shell(shell_ref.at[half], [held[half, x] for x in range(8)], x_ref[half], pick_ref[...])
    own_conv(lambda half, x: held[half, x], w_ref, part_ref, wide, block)


def second_own_kernel(hidden_ref, x_ref, pick_ref, w_ref, part_ref, shell_ref, wide, block):
    plane = lambda ref: lambda half, x: ref[half, x * 64 : x * 64 + 64, :].astype(jnp.float32)
    for half in range(2):
        planes = [plane(hidden_ref)(half, x) for x in range(8)]
        store_shell(shell_ref.at[half], planes, hidden_ref[half], pick_ref[...])
    own_conv(plane(hidden_ref), w_ref, part_ref, wide, block, plane(x_ref))


def fill_pool(pool, start, source):
    for entry in range(source.shape[0]):
        pool[start + entry] = source[entry].astype(jnp.float32)


def build_face(face, src_ref, pool, halo):
    first, last = edge_masks()
    delta, cell, z_cell = ((0, 7, 7), (2, 0, 0))[face % 2]

    def entry(brick, k):
        ref = src_ref[brick, k]
        return jnp.where(ref < 0, BLANK, ref)

    def put(pair, outer, parts):
        lanes = slice((outer % 2) * 128, (outer % 2) * 128 + 128)
        for shift in range(3):
            both = jnp.concatenate([parts[0][shift], parts[1][shift]], axis=0)
            halo[face, shift, outer // 2, pair * 16 : pair * 16 + 16, lanes] = both.astype(jnp.bfloat16)

    def column(around, x, y):
        below, here, above = around
        start, at_lo, at_hi = ring_row(x, y), cell_row(x, y, 7), cell_row(x, y, 0)
        mid = pool[here, start : start + 8, :]
        lo = jnp.broadcast_to(pool[below, at_lo : at_lo + 1, :], (8, 128))
        hi = jnp.broadcast_to(pool[above, at_hi : at_hi + 1, :], (8, 128))
        return shift_down(mid, first, lo), mid, shift_up(mid, last, hi)

    def z_plane(here, x):
        if x in (0, 7):
            mid = pool[here, pl.ds(ring_row(x, 0) + z_cell, 8, stride=8), :]
        else:
            start = cell_row(x, 1, z_cell) - 1
            at_lo, at_hi = cell_row(x, 0, z_cell), cell_row(x, 7, z_cell)
            mid = pool[here, start : start + 8, :]
            mid = jnp.where(first, jnp.broadcast_to(pool[here, at_lo : at_lo + 1, :], (8, 128)), mid)
            mid = jnp.where(last, jnp.broadcast_to(pool[here, at_hi : at_hi + 1, :], (8, 128)), mid)
        return shift_down(mid, first, 0.0), mid, shift_up(mid, last, 0.0)

    for pair in range(BR // 2):
        bricks = (2 * pair, 2 * pair + 1)
        if face < 2:
            around = [[[entry(b, delta * 9 + dy * 3 + dz) for dz in range(3)] for dy in range(3)] for b in bricks]
            for outer in range(10):
                dy = 0 if outer == 0 else (2 if outer == 9 else 1)
                y = 7 if outer == 0 else (0 if outer == 9 else outer - 1)
                put(pair, outer, [column(around[half][dy], cell, y) for half in range(2)])
        elif face < 4:
            around = [[entry(b, 9 + delta * 3 + dz) for dz in range(3)] for b in bricks]
            for x in range(8):
                put(pair, x + 1, [column(around[half], x, cell) for half in range(2)])
        else:
            here = [entry(b, 12 + delta) for b in bricks]
            for x in range(8):
                put(pair, x + 1, [z_plane(here[half], x) for half in range(2)])


def halo_weights(w_ref, along):
    for face in range(2):
        end = 2 * face
        for shift in range(3):
            toeplitz(along.at[face, shift], [w_ref[end * 9 + tap * 3 + shift] for tap in range(3)])
            toeplitz(along.at[2 + face, shift], [w_ref[tap * 9 + end * 3 + shift] for tap in range(3)])
            toeplitz(along.at[4 + face, shift], [w_ref[tap * 9 + shift * 3 + end] for tap in range(3)])


def sum_face(face, halo, along, sums):
    rows = 8 * BR
    acc = jnp.zeros((4 * rows, 256), jnp.float32)
    for shift in range(3):
        for side in range(2):
            part = halo[face, shift, side : side + 4].reshape(4 * rows, 256)
            acc = acc + jnp.dot(part, along[face, shift, side], preferred_element_type=jnp.float32)
    sums[face] = acc.reshape(4, BR, 8, 256)


def halo_part(src_ref, sources, landed, sems, streams, stream_sems, pool, halo, along, sums):
    loads = start_all([pltpu.make_async_copy(a, b, sems.at[n]) for n, (a, b) in enumerate(zip(sources, landed))])
    pool[BLANK] = jnp.zeros((SHELL, 128), jnp.float32)
    for face in range(2, 6):
        for shift in range(3):
            halo[face, shift, 0, :, 0:128] = jnp.zeros((8 * BR, 128), jnp.bfloat16)
            halo[face, shift, 4, :, 128:256] = jnp.zeros((8 * BR, 128), jnp.bfloat16)
    loads[0].wait()
    halo_weights(landed[0], along)
    for load, start, field in zip(loads[1:], (0, BR, BR + EDGE, BR + 2 * EDGE), landed[1:]):
        load.wait()
        if field is landed[-1]:
            start_streams(streams, stream_sems)
        fill_pool(pool, start, field)

    build_face(0, src_ref, pool, halo)
    for face in range(6):
        if face < 5:
            build_face(face + 1, src_ref, pool, halo)
        sum_face(face, halo, along, sums)


def start_streams(streams, stream_sems):
    for pair in range(BR // 2):
        for n, (source, target, size) in enumerate(streams):
            at = pl.ds(pair * size, size)
            pltpu.make_async_copy(source.at[at], target.at[at], stream_sems.at[n, pair]).start()


def wait_stream(streams, stream_sems, pair):
    for n, (source, target, size) in enumerate(streams):
        at = pl.ds(pair * size, size)
        pltpu.make_async_copy(source.at[at], target.at[at], stream_sems.at[n, pair]).wait()


def whole_plane(part, sums, pair, half, x):
    first, last = edge_masks()
    brick = pair * 2 + half
    lanes = slice((x % 2) * 128, (x % 2) * 128 + 128)
    columns = []
    for y in range(8):
        row = (x // 2) * 128 + y * 16 + half * 8
        value = part[pair, row : row + 8, lanes]
        if x in (0, 7):
            value = value + sums[x // 7, y // 2, brick, :, (y % 2) * 128 : (y % 2) * 128 + 128]
        if y in (0, 7):
            value = value + sums[2 + y // 7, x // 2, brick, :, lanes]
        lo = jnp.broadcast_to(sums[4, x // 2, brick, y : y + 1, lanes], (8, 128))
        hi = jnp.broadcast_to(sums[5, x // 2, brick, y : y + 1, lanes], (8, 128))
        columns.append(value + jnp.where(first, lo, jnp.where(last, hi, 0.0)))
    return jnp.concatenate(columns, axis=0)


def first_halo_kernel(
    src_ref, send_ref, pick_ref, part_ref, mask_ref, w_ref, shells_ref, before_ref, after_ref, recv_ref,
    hidden_ref, out_ref, low_ref, high_ref,
    pool, halo, along, sums, w, shells, before, after, recv, part, mask, done, sems, stream_sems, done_sems,
    own, out_sems,
):
    streams = ((part_ref, part, 1), (mask_ref, mask, 2))
    sources = (w_ref, shells_ref, before_ref, after_ref, recv_ref)
    landed = (w, shells, before, after, recv)
    halo_part(src_ref, sources, landed, sems, streams, stream_sems, pool, halo, along, sums)

    def store(pair):
        at = pl.ds(pair * 2, 2)
        return pltpu.make_async_copy(done.at[at], hidden_ref.at[at], done_sems.at[pair])

    def pair_body(pair, carry):
        wait_stream(streams, stream_sems, pair)
        for half in range(2):
            brick = pair * 2 + half
            planes = []
            for x in range(8):
                rows = slice(x * 64, x * 64 + 64)
                value = whole_plane(part, sums, pair, half, x)
                value = value / (1.0 + jnp.exp(-value)) * mask[brick, rows, :].astype(jnp.float32)
                done[brick, rows, :] = value.astype(jnp.bfloat16)
                planes.append(value)
            store_shell(own.at[brick], planes)
        store(pair).start()
        return carry

    lax.fori_loop(0, BR // 2, pair_body, 0)
    for brick in range(0, BR, 2):
        both = jnp.concatenate([done[brick], done[brick + 1]], axis=1)
        inner = jnp.dot(pick_ref[...], both, preferred_element_type=jnp.float32).astype(jnp.bfloat16)
        own[brick, FACE_LO:SHELL, :] = inner[:, :128]
        own[brick + 1, FACE_LO:SHELL, :] = inner[:, 128:]
    copies = hand_out(send_ref, own, out_ref, low_ref, high_ref, out_sems)
    wait_all([store(pair) for pair in range(BR // 2)])
    wait_all(copies)


def second_halo_kernel(
    src_ref, part_ref, mask_ref, w_ref, shells_ref, before_ref, after_ref, recv_ref,
    result_ref,
    pool, halo, along, sums, w, shells, before, after, recv, part, mask, done, sems, stream_sems, done_sems,
):
    streams = ((part_ref, part, 1), (mask_ref, mask, 2))
    sources = (w_ref, shells_ref, before_ref, after_ref, recv_ref)
    landed = (w, shells, before, after, recv)
    halo_part(src_ref, sources, landed, sems, streams, stream_sems, pool, halo, along, sums)

    def store(pair):
        at = pl.ds(pair * 2, 2)
        return pltpu.make_async_copy(done.at[at], result_ref.at[at], done_sems.at[pair])

    def pair_body(pair, carry):
        wait_stream(streams, stream_sems, pair)
        for half in range(2):
            brick = pair * 2 + half
            for x in range(8):
                rows = slice(x * 64, x * 64 + 64)
                value = whole_plane(part, sums, pair, half, x)
                done[brick, rows, :] = (value * mask[brick, rows, :].astype(jnp.float32)).astype(jnp.bfloat16)
        store(pair).start()
        return carry

    lax.fori_loop(0, BR // 2, pair_body, 0)
    wait_all([store(pair) for pair in range(BR // 2)])


WHOLE = functools.partial(pl.BlockSpec, memory_space=pltpu.VMEM)
SCALARS = functools.partial(pl.BlockSpec, memory_space=pltpu.SMEM)
ANYWHERE = functools.partial(pl.BlockSpec, memory_space=pl.ANY)
GRID = (BR // 2,)
FIELD = jax.ShapeDtypeStruct((BR, 512, 128), jnp.bfloat16)
PARTIAL = jax.ShapeDtypeStruct((BR // 2, 512, 256), jnp.float32)


def pair_spec():
    return pl.BlockSpec((2, 512, 128), lambda i: (i, 0, 0))


def part_spec():
    return pl.BlockSpec((1, 512, 256), lambda i: (i, 0, 0))


def shell_pair_spec():
    return pl.BlockSpec((2, SHELL, 128), lambda i: (i, 0, 0))


def shells_of(*counts):
    return [jax.ShapeDtypeStruct((n, SHELL, 128), jnp.bfloat16) for n in counts]


def params():
    return pltpu.CompilerParams(vmem_limit_bytes=VMEM_LIMIT)


def own_scratch():
    return [pltpu.VMEM((9, 2, 256, 256), jnp.bfloat16), pltpu.VMEM((3, 5, 10, 16, 256), jnp.bfloat16)]


def halo_scratch():
    shells = [pltpu.VMEM((n, SHELL, 128), jnp.bfloat16) for n in (BR, EDGE, EDGE, SLOTS)]
    return [
        pltpu.VMEM((ENTRIES + 1, SHELL, 128), jnp.float32),
        pltpu.VMEM((6, 3, 5, 8 * BR, 256), jnp.bfloat16),
        pltpu.VMEM((6, 3, 2, 256, 256), jnp.bfloat16),
        pltpu.VMEM((6, 4, BR, 8, 256), jnp.float32),
        pltpu.VMEM((27, 128, 128), jnp.bfloat16),
        *shells,
        pltpu.VMEM((BR // 2, 512, 256), jnp.float32),
        pltpu.VMEM((BR, 512, 128), jnp.bfloat16),
        pltpu.VMEM((BR, 512, 128), jnp.bfloat16),
        pltpu.SemaphoreType.DMA((5,)),
        pltpu.SemaphoreType.DMA((2, BR // 2)),
        pltpu.SemaphoreType.DMA((BR // 2,)),
    ]


def own_shells_scratch():
    return [pltpu.VMEM((BR, SHELL, 128), jnp.bfloat16), pltpu.SemaphoreType.DMA((SLOTS + 2,))]


OWN_COST = pl.CostEstimate(flops=2 * 6 * 512 * 4608 * 256, bytes_accessed=8 * MIB, transcendentals=0)
HALO_COST = pl.CostEstimate(flops=2 * 36 * 384 * 256 * 256, bytes_accessed=10 * MIB, transcendentals=0)


def pack(send, feats, occ, pick):
    return pl.pallas_call(
        pack_kernel,
        in_specs=[SCALARS(), ANYWHERE(), WHOLE(), ANYWHERE()],
        out_specs=[ANYWHERE()] * 3,
        out_shape=shells_of(SLOTS, EDGE, EDGE),
        scratch_shapes=[
            pltpu.VMEM((BR, 512, 128), jnp.bfloat16),
            pltpu.VMEM((BR, SHELL, 128), jnp.bfloat16),
            pltpu.VMEM((SHELL, 512), jnp.bfloat16),
            pltpu.SemaphoreType.DMA((BR // 2 + 1,)),
            pltpu.SemaphoreType.DMA((SLOTS + 2,)),
        ],
        compiler_params=params(),
        name="pack_shells",
    )(send, feats, occ, pick)


def first_own(feats, occ, pick, weights):
    return pl.pallas_call(
        first_own_kernel,
        grid=GRID,
        in_specs=[pair_spec(), WHOLE(), WHOLE(), WHOLE()],
        out_specs=[part_spec(), pair_spec(), pair_spec(), shell_pair_spec()],
        out_shape=[PARTIAL, FIELD, FIELD] + shells_of(BR),
        scratch_shapes=own_scratch(),
        compiler_params=params(),
        cost_estimate=OWN_COST,
        name="first_own",
    )(feats, occ, pick, weights)


def second_own(hidden, x, pick, weights):
    return pl.pallas_call(
        second_own_kernel,
        grid=GRID,
        in_specs=[pair_spec(), pair_spec(), WHOLE(), WHOLE()],
        out_specs=[part_spec(), shell_pair_spec()],
        out_shape=[PARTIAL] + shells_of(BR),
        scratch_shapes=own_scratch(),
        compiler_params=params(),
        cost_estimate=OWN_COST,
        name="second_own",
    )(hidden, x, pick, weights)


def first_halo(src, send, pick, part, mask, weights, shells, before, after, recv):
    return pl.pallas_call(
        first_halo_kernel,
        in_specs=[SCALARS(), SCALARS(), WHOLE()] + [ANYWHERE()] * 7,
        out_specs=[ANYWHERE()] * 4,
        out_shape=[FIELD] + shells_of(SLOTS, EDGE, EDGE),
        scratch_shapes=halo_scratch() + own_shells_scratch(),
        compiler_params=params(),
        cost_estimate=HALO_COST,
        name="first_halo",
    )(src, send, pick, part, mask, weights, shells, before, after, recv)


def second_halo(src, part, mask, weights, shells, before, after, recv):
    return pl.pallas_call(
        second_halo_kernel,
        in_specs=[SCALARS()] + [ANYWHERE()] * 7,
        out_specs=ANYWHERE(),
        out_shape=FIELD,
        scratch_shapes=halo_scratch(),
        compiler_params=params(),
        cost_estimate=HALO_COST,
        name="second_halo",
    )(src, part, mask, weights, shells, before, after, recv)


def shifted(value, axis, steps):
    count = lax.axis_size(axis)
    initial, last = (max(0, -steps), min(count, count - steps))
    return lax.ppermute(value, axis, [(source, source + steps) for source in range(initial, last)])


def exchange(outgoing, low, high):
    arrived = lax.all_to_all(outgoing, "dev", split_axis=0, concat_axis=0, tiled=True)
    before = shifted(low, ("grp", "dev"), 1)
    after = shifted(high, ("grp", "dev"), -1)
    return before, after, arrived


def per_device(features, occupancy, w_first, w_second, src_ref, send_list):
    send = send_list.reshape(SLOTS)
    pick = shell_matrix()
    outgoing, low, high = pack(send, features, occupancy, pick)
    pick = pick[FACE_LO:]
    around = exchange(outgoing, low, high)
    part, x, mask, shells = first_own(features, occupancy, pick, w_first)
    hidden, outgoing, low, high = first_halo(src_ref, send, pick, part, mask, w_first, shells, *around)
    around = exchange(outgoing, low, high)
    part, shells = second_own(hidden, x, pick, w_second)
    return second_halo(src_ref, part, mask, w_second, shells, *around)


def solution(mesh):
    placed = (
        P(("grp", "dev"), None, None),
        P(("grp", "dev"), None),
        P(),
        P(),
        P(("grp", "dev"), None),
        P(("grp", "dev"), None, None),
    )
    return jax.shard_map(
        per_device,
        mesh=mesh,
        in_specs=placed,
        out_specs=P(("grp", "dev"), None, None),
        check_vma=False,
    )
```

```python
import functools

import jax
import jax.numpy as jnp
import numpy as np
from jax import lax
from jax.experimental import pallas as pl
from jax.experimental.pallas import tpu as pltpu
from jax.sharding import PartitionSpec as P

BR = 12
EDGE = 2
SLOTS = 16
ENTRIES = BR + 2 * EDGE + SLOTS
BLANK = ENTRIES
SHELL = 304
FACE_LO = 224
FACE_HI = 260
MIB = 1024 * 1024
VMEM_LIMIT = 64 * MIB - 96 * 1024


def ring_row(x, y):
    if x == 0:
        return y * 8
    if x == 7:
        return 64 + y * 8
    if y == 0:
        return 128 + (x - 1) * 8
    if y == 7:
        return 176 + (x - 1) * 8
    return None


def cell_row(x, y, z):
    first = ring_row(x, y)
    if first is not None:
        return first + z
    return (FACE_LO if z == 0 else FACE_HI) + (x - 1) * 6 + (y - 1)


def shell_matrix():
    picked = np.zeros((SHELL, 512), np.float32)
    for x in range(8):
        for y in range(8):
            for z in range(8):
                cell = x * 64 + y * 8 + z
                first = ring_row(x, y)
                if first is not None:
                    picked[first + z, cell] = 1
                elif z in (0, 7):
                    picked[cell_row(x, y, z), cell] = 1
    return jnp.asarray(picked, jnp.bfloat16)


def store_shell(shell, planes):
    shell[0:64, :] = planes[0].astype(jnp.bfloat16)
    shell[64:128, :] = planes[7].astype(jnp.bfloat16)
    for x in (1, 3, 5):
        for start, rows in ((128, slice(0, 8)), (176, slice(56, 64))):
            both = jnp.concatenate([planes[x][rows], planes[x + 1][rows]], axis=0)
            shell[start + (x - 1) * 8 : start + (x + 1) * 8, :] = both.astype(jnp.bfloat16)


def store_inner(shell, planes, cells, inner):
    for x in range(1, 7):
        rows = (x - 1) * 6
        cells[x * 64 : x * 64 + 64, :] = planes[x]
        inner[rows : rows + 6, :] = cells[pl.ds(x * 64 + 8, 6, stride=8), :]
        inner[rows + 36 : rows + 42, :] = cells[pl.ds(x * 64 + 15, 6, stride=8), :]
    inner[72:80, :] = jnp.zeros((8, 128), jnp.float32)
    shell[FACE_LO:SHELL, :] = inner[...].astype(jnp.bfloat16)


def parity():
    return lax.rem(lax.axis_index("dev"), 2)


def start_all(copies):
    for copy in copies:
        copy.start()
    return copies


def wait_all(copies):
    for copy in copies:
        copy.wait()


def hand_out(send_ref, odd, own, out_ref, near_ref, far_ref, sems):
    first, second = jnp.where(odd == 0, BR - EDGE, 0), jnp.where(odd == 0, 0, BR - EDGE)
    copies = [pltpu.make_async_copy(own.at[pl.ds(first, EDGE)], near_ref, sems.at[SLOTS])]
    copies.append(pltpu.make_async_copy(own.at[pl.ds(second, EDGE)], far_ref, sems.at[SLOTS + 1]))
    for slot in range(SLOTS):
        brick = jnp.maximum(send_ref[slot], 0)
        copies.append(pltpu.make_async_copy(own.at[brick], out_ref.at[slot], sems.at[slot]))
    return start_all(copies)


def pack_kernel(
    send_ref, feat_ref, occ_ref, pick_ref, out_ref, near_ref, far_ref, feats, own, pick, in_sems, out_sems
):
    pick_load = pltpu.make_async_copy(pick_ref, pick, in_sems.at[BR // 2])
    pick_load.start()
    pairs = [pl.ds(pair * 2, 2) for pair in range(BR // 2)]
    loads = start_all(
        [pltpu.make_async_copy(feat_ref.at[at], feats.at[at], in_sems.at[n]) for n, at in enumerate(pairs)]
    )
    pick_load.wait()
    for part in range(0, BR // 2, 3):
        wait_all(loads[part : part + 3])
        for brick in range(2 * part, 2 * part + 6):
            held = occ_ref[brick : brick + 1, :].astype(jnp.float32).astype(jnp.bfloat16)
            chooser = pick[...] * jnp.broadcast_to(held, (SHELL, 512))
            shell = jnp.dot(chooser, feats[brick], preferred_element_type=jnp.float32)
            own[brick] = shell.astype(jnp.bfloat16)
    wait_all(hand_out(send_ref, parity(), own, out_ref, near_ref, far_ref, out_sems))


def toeplitz(target, taps):
    t0, t1, t2 = taps
    zero = jnp.zeros((128, 128), jnp.bfloat16)
    target[0, 0:128, 0:128] = t0
    target[0, 0:128, 128:256] = zero
    target[0, 128:256, 0:128] = t1
    target[0, 128:256, 128:256] = t0
    target[1, 0:128, 0:128] = t2
    target[1, 0:128, 128:256] = t1
    target[1, 128:256, 0:128] = zero
    target[1, 128:256, 128:256] = t2


def edge_masks():
    sub = lax.broadcasted_iota(jnp.int32, (8, 128), 0)
    return sub == 0, sub == 7


def shift_down(value, first, fill):
    return jnp.where(first, fill, pltpu.roll(value, 1, 0))


def shift_up(value, last, fill):
    return jnp.where(last, fill, pltpu.roll(value, 7, 0))


def own_conv(plane, w_ref, part_ref, wide, block, base=None):
    step = pl.program_id(0)

    @pl.when(step == 0)
    def _():
        block[...] = jnp.zeros_like(block)
        for tap in range(9):
            toeplitz(wide.at[tap], (w_ref[tap], w_ref[9 + tap], w_ref[18 + tap]))

    first, last = edge_masks()
    for x in range(8):
        planes = [plane(half, x) for half in range(2)]
        px = x + 1
        lanes = slice((px % 2) * 128, (px % 2) * 128 + 128)
        for y in range(8):
            mids = [planes[half][y * 8 : y * 8 + 8] for half in range(2)]
            for az, parts in enumerate(
                (
                    [shift_down(mid, first, 0.0) for mid in mids],
                    mids,
                    [shift_up(mid, last, 0.0) for mid in mids],
                )
            ):
                block[az, px // 2, y + 1, :, lanes] = jnp.concatenate(parts, axis=0).astype(jnp.bfloat16)
    acc = jnp.zeros((512, 256), jnp.float32)
    for az in range(3):
        for ay in range(3):
            for side in range(2):
                part = block[az, side : side + 4, ay : ay + 8].reshape(512, 256)
                acc = acc + jnp.dot(part, wide[ay * 3 + az, side], preferred_element_type=jnp.float32)
    if base is None:
        part_ref[0] = acc
        return
    for half in range(2):
        for x in range(8):
            added = base(half, x)
            lanes = slice((x % 2) * 128, (x % 2) * 128 + 128)
            for y in range(8):
                row = (x // 2) * 128 + y * 16 + half * 8
                part_ref[0, row : row + 8, lanes] = acc[row : row + 8, lanes] + added[y * 8 : y * 8 + 8]


def first_own_kernel(feat_ref, occ_ref, w_ref, part_ref, x_ref, mask_ref, shell_ref, wide, block, cells, inner):
    step = pl.program_id(0)
    rows = lax.broadcasted_iota(jnp.int32, (128, 128), 0)
    cols = lax.broadcasted_iota(jnp.int32, (128, 128), 1)
    diagonal = rows == cols
    ones = jnp.ones((128, 128), jnp.bfloat16)
    held = {}
    for half in range(2):
        occupied = occ_ref[pl.ds(step * 2 + half, 1), :].astype(jnp.float32)
        for chunk in range(4):
            at = slice(chunk * 128, chunk * 128 + 128)
            scale = jnp.where(diagonal, jnp.broadcast_to(occupied[:, at], (128, 128)), 0.0).astype(jnp.bfloat16)
            right = jnp.concatenate([feat_ref[half, at, :], ones], axis=1)
            both = jnp.dot(scale, right, preferred_element_type=jnp.float32)
            x_ref[half, at, :] = both[:, :128].astype(jnp.bfloat16)
            mask_ref[half, at, :] = both[:, 128:].astype(jnp.bfloat16)
            held[half, 2 * chunk] = both[:64, :128]
            held[half, 2 * chunk + 1] = both[64:, :128]
        planes = [held[half, x] for x in range(8)]
        store_shell(shell_ref.at[half], planes)
        store_inner(shell_ref.at[half], planes, cells.at[half], inner.at[half])
    own_conv(lambda half, x: held[half, x], w_ref, part_ref, wide, block)


def second_own_kernel(hidden_ref, x_ref, w_ref, part_ref, shell_ref, wide, block, cells, inner):
    plane = lambda ref: lambda half, x: ref[half, x * 64 : x * 64 + 64, :].astype(jnp.float32)
    for half in range(2):
        planes = [plane(hidden_ref)(half, x) for x in range(8)]
        store_shell(shell_ref.at[half], planes)
        store_inner(shell_ref.at[half], planes, cells.at[half], inner.at[half])
    own_conv(plane(hidden_ref), w_ref, part_ref, wide, block, plane(x_ref))


def fill_pool(pool, start, source):
    for entry in range(source.shape[0]):
        pool[start + entry] = source[entry].astype(jnp.float32)


def build_face(face, src_ref, pool, halo):
    first, last = edge_masks()
    delta, cell, z_cell = ((0, 7, 7), (2, 0, 0))[face % 2]

    def entry(brick, k):
        ref = src_ref[brick, k]
        return jnp.where(ref < 0, BLANK, ref)

    def put(pair, outer, parts):
        lanes = slice((outer % 2) * 128, (outer % 2) * 128 + 128)
        for shift in range(3):
            both = jnp.concatenate([parts[0][shift], parts[1][shift]], axis=0)
            halo[face, shift, outer // 2, pair * 16 : pair * 16 + 16, lanes] = both.astype(jnp.bfloat16)

    def column(around, x, y):
        below, here, above = around
        start, at_lo, at_hi = ring_row(x, y), cell_row(x, y, 7), cell_row(x, y, 0)
        mid = pool[here, start : start + 8, :]
        lo = jnp.broadcast_to(pool[below, at_lo : at_lo + 1, :], (8, 128))
        hi = jnp.broadcast_to(pool[above, at_hi : at_hi + 1, :], (8, 128))
        return shift_down(mid, first, lo), mid, shift_up(mid, last, hi)

    def z_plane(here, x):
        if x in (0, 7):
            mid = pool[here, pl.ds(ring_row(x, 0) + z_cell, 8, stride=8), :]
        else:
            start = cell_row(x, 1, z_cell) - 1
            at_lo, at_hi = cell_row(x, 0, z_cell), cell_row(x, 7, z_cell)
            mid = pool[here, start : start + 8, :]
            mid = jnp.where(first, jnp.broadcast_to(pool[here, at_lo : at_lo + 1, :], (8, 128)), mid)
            mid = jnp.where(last, jnp.broadcast_to(pool[here, at_hi : at_hi + 1, :], (8, 128)), mid)
        return shift_down(mid, first, 0.0), mid, shift_up(mid, last, 0.0)

    for pair in range(BR // 2):
        bricks = (2 * pair, 2 * pair + 1)
        if face < 2:
            around = [[[entry(b, delta * 9 + dy * 3 + dz) for dz in range(3)] for dy in range(3)] for b in bricks]
            for outer in range(10):
                dy = 0 if outer == 0 else (2 if outer == 9 else 1)
                y = 7 if outer == 0 else (0 if outer == 9 else outer - 1)
                put(pair, outer, [column(around[half][dy], cell, y) for half in range(2)])
        elif face < 4:
            around = [[entry(b, 9 + delta * 3 + dz) for dz in range(3)] for b in bricks]
            for x in range(8):
                put(pair, x + 1, [column(around[half], x, cell) for half in range(2)])
        else:
            here = [entry(b, 12 + delta) for b in bricks]
            for x in range(8):
                put(pair, x + 1, [z_plane(here[half], x) for half in range(2)])


def halo_weights(w_ref, along):
    for face in range(2):
        end = 2 * face
        for shift in range(3):
            toeplitz(along.at[face, shift], [w_ref[end * 9 + tap * 3 + shift] for tap in range(3)])
            toeplitz(along.at[2 + face, shift], [w_ref[tap * 9 + end * 3 + shift] for tap in range(3)])
            toeplitz(along.at[4 + face, shift], [w_ref[tap * 9 + shift * 3 + end] for tap in range(3)])


def sum_face(face, halo, along, sums):
    rows = 8 * BR
    acc = jnp.zeros((4 * rows, 256), jnp.float32)
    for shift in range(3):
        for side in range(2):
            part = halo[face, shift, side : side + 4].reshape(4 * rows, 256)
            acc = acc + jnp.dot(part, along[face, shift, side], preferred_element_type=jnp.float32)
    sums[face] = acc.reshape(4, BR, 8, 256)


def halo_part(odd, src_ref, sources, landed, sems, streams, stream_sems, pool, halo, along, sums):
    loads = start_all([pltpu.make_async_copy(a, b, sems.at[n]) for n, (a, b) in enumerate(zip(sources, landed))])
    pool[BLANK] = jnp.zeros((SHELL, 128), jnp.float32)
    for face in range(2, 6):
        for shift in range(3):
            halo[face, shift, 0, :, 0:128] = jnp.zeros((8 * BR, 128), jnp.bfloat16)
            halo[face, shift, 4, :, 128:256] = jnp.zeros((8 * BR, 128), jnp.bfloat16)
    near, far = BR + EDGE * (1 - odd), BR + EDGE * odd
    loads[0].wait()
    halo_weights(landed[0], along)
    for load, start, field in zip(loads[1:], (0, near, far, BR + 2 * EDGE), landed[1:]):
        load.wait()
        if field is landed[-1]:
            start_streams(streams, stream_sems)
        fill_pool(pool, start, field)

    build_face(0, src_ref, pool, halo)
    for face in range(6):
        if face < 5:
            build_face(face + 1, src_ref, pool, halo)
        sum_face(face, halo, along, sums)


def start_streams(streams, stream_sems):
    for pair in range(BR // 2):
        for n, (source, target, size) in enumerate(streams):
            at = pl.ds(pair * size, size)
            pltpu.make_async_copy(source.at[at], target.at[at], stream_sems.at[n, pair]).start()


def wait_stream(streams, stream_sems, pair):
    for n, (source, target, size) in enumerate(streams):
        at = pl.ds(pair * size, size)
        pltpu.make_async_copy(source.at[at], target.at[at], stream_sems.at[n, pair]).wait()


def whole_plane(part, sums, pair, half, x):
    first, last = edge_masks()
    brick = pair * 2 + half
    lanes = slice((x % 2) * 128, (x % 2) * 128 + 128)
    columns = []
    for y in range(8):
        row = (x // 2) * 128 + y * 16 + half * 8
        value = part[pair, row : row + 8, lanes]
        if x in (0, 7):
            value = value + sums[x // 7, y // 2, brick, :, (y % 2) * 128 : (y % 2) * 128 + 128]
        if y in (0, 7):
            value = value + sums[2 + y // 7, x // 2, brick, :, lanes]
        lo = jnp.broadcast_to(sums[4, x // 2, brick, y : y + 1, lanes], (8, 128))
        hi = jnp.broadcast_to(sums[5, x // 2, brick, y : y + 1, lanes], (8, 128))
        columns.append(value + jnp.where(first, lo, jnp.where(last, hi, 0.0)))
    return jnp.concatenate(columns, axis=0)


def first_halo_kernel(
    src_ref, send_ref, pick_ref, part_ref, mask_ref, w_ref, shells_ref, near_in_ref, far_in_ref, recv_ref,
    hidden_ref, out_ref, near_ref, far_ref,
    pool, halo, along, sums, w, shells, near, far, recv, part, mask, done, sems, stream_sems, done_sems,
    own, out_sems,
):
    streams = ((part_ref, part, 1), (mask_ref, mask, 2))
    sources = (w_ref, shells_ref, near_in_ref, far_in_ref, recv_ref)
    landed = (w, shells, near, far, recv)
    halo_part(parity(), src_ref, sources, landed, sems, streams, stream_sems, pool, halo, along, sums)

    def store(pair):
        at = pl.ds(pair * 2, 2)
        return pltpu.make_async_copy(done.at[at], hidden_ref.at[at], done_sems.at[pair])

    def pair_body(pair, carry):
        wait_stream(streams, stream_sems, pair)
        for half in range(2):
            brick = pair * 2 + half
            planes = []
            for x in range(8):
                rows = slice(x * 64, x * 64 + 64)
                value = whole_plane(part, sums, pair, half, x)
                value = value / (1.0 + jnp.exp(-value)) * mask[brick, rows, :].astype(jnp.float32)
                done[brick, rows, :] = value.astype(jnp.bfloat16)
                planes.append(value)
            store_shell(own.at[brick], planes)
        store(pair).start()
        return carry

    lax.fori_loop(0, BR // 2, pair_body, 0)
    for brick in range(0, BR, 2):
        both = jnp.concatenate([done[brick], done[brick + 1]], axis=1)
        inner = jnp.dot(pick_ref[...], both, preferred_element_type=jnp.float32).astype(jnp.bfloat16)
        own[brick, FACE_LO:SHELL, :] = inner[:, :128]
        own[brick + 1, FACE_LO:SHELL, :] = inner[:, 128:]
    copies = hand_out(send_ref, parity(), own, out_ref, near_ref, far_ref, out_sems)
    wait_all([store(pair) for pair in range(BR // 2)])
    wait_all(copies)


def second_halo_kernel(
    src_ref, part_ref, mask_ref, w_ref, shells_ref, near_in_ref, far_in_ref, recv_ref,
    result_ref,
    pool, halo, along, sums, w, shells, near, far, recv, part, mask, done, sems, stream_sems, done_sems,
):
    streams = ((part_ref, part, 1), (mask_ref, mask, 2))
    sources = (w_ref, shells_ref, near_in_ref, far_in_ref, recv_ref)
    landed = (w, shells, near, far, recv)
    halo_part(parity(), src_ref, sources, landed, sems, streams, stream_sems, pool, halo, along, sums)

    def store(pair):
        at = pl.ds(pair * 2, 2)
        return pltpu.make_async_copy(done.at[at], result_ref.at[at], done_sems.at[pair])

    def pair_body(pair, carry):
        wait_stream(streams, stream_sems, pair)
        for half in range(2):
            brick = pair * 2 + half
            for x in range(8):
                rows = slice(x * 64, x * 64 + 64)
                value = whole_plane(part, sums, pair, half, x)
                done[brick, rows, :] = (value * mask[brick, rows, :].astype(jnp.float32)).astype(jnp.bfloat16)
        store(pair).start()
        return carry

    lax.fori_loop(0, BR // 2, pair_body, 0)
    wait_all([store(pair) for pair in range(BR // 2)])


WHOLE = functools.partial(pl.BlockSpec, memory_space=pltpu.VMEM)
SCALARS = functools.partial(pl.BlockSpec, memory_space=pltpu.SMEM)
ANYWHERE = functools.partial(pl.BlockSpec, memory_space=pl.ANY)
GRID = (BR // 2,)
FIELD = jax.ShapeDtypeStruct((BR, 512, 128), jnp.bfloat16)
PARTIAL = jax.ShapeDtypeStruct((BR // 2, 512, 256), jnp.float32)


def pair_spec():
    return pl.BlockSpec((2, 512, 128), lambda i: (i, 0, 0))


def part_spec():
    return pl.BlockSpec((1, 512, 256), lambda i: (i, 0, 0))


def shell_pair_spec():
    return pl.BlockSpec((2, SHELL, 128), lambda i: (i, 0, 0))


def shells_of(*counts):
    return [jax.ShapeDtypeStruct((n, SHELL, 128), jnp.bfloat16) for n in counts]


def params():
    return pltpu.CompilerParams(vmem_limit_bytes=VMEM_LIMIT)


def own_scratch():
    return [
        pltpu.VMEM((9, 2, 256, 256), jnp.bfloat16),
        pltpu.VMEM((3, 5, 10, 16, 256), jnp.bfloat16),
        pltpu.VMEM((2, 512, 128), jnp.float32),
        pltpu.VMEM((2, SHELL - FACE_LO, 128), jnp.float32),
    ]


def halo_scratch():
    shells = [pltpu.VMEM((n, SHELL, 128), jnp.bfloat16) for n in (BR, EDGE, EDGE, SLOTS)]
    return [
        pltpu.VMEM((ENTRIES + 1, SHELL, 128), jnp.float32),
        pltpu.VMEM((6, 3, 5, 8 * BR, 256), jnp.bfloat16),
        pltpu.VMEM((6, 3, 2, 256, 256), jnp.bfloat16),
        pltpu.VMEM((6, 4, BR, 8, 256), jnp.float32),
        pltpu.VMEM((27, 128, 128), jnp.bfloat16),
        *shells,
        pltpu.VMEM((BR // 2, 512, 256), jnp.float32),
        pltpu.VMEM((BR, 512, 128), jnp.bfloat16),
        pltpu.VMEM((BR, 512, 128), jnp.bfloat16),
        pltpu.SemaphoreType.DMA((5,)),
        pltpu.SemaphoreType.DMA((2, BR // 2)),
        pltpu.SemaphoreType.DMA((BR // 2,)),
    ]


def own_shells_scratch():
    return [pltpu.VMEM((BR, SHELL, 128), jnp.bfloat16), pltpu.SemaphoreType.DMA((SLOTS + 2,))]


OWN_COST = pl.CostEstimate(flops=2 * 6 * 512 * 4608 * 256, bytes_accessed=8 * MIB, transcendentals=0)
HALO_COST = pl.CostEstimate(flops=2 * 36 * 384 * 256 * 256, bytes_accessed=10 * MIB, transcendentals=0)


def pack(send, feats, occ, pick):
    return pl.pallas_call(
        pack_kernel,
        in_specs=[SCALARS(), ANYWHERE(), WHOLE(), ANYWHERE()],
        out_specs=[ANYWHERE()] * 3,
        out_shape=shells_of(SLOTS, EDGE, EDGE),
        scratch_shapes=[
            pltpu.VMEM((BR, 512, 128), jnp.bfloat16),
            pltpu.VMEM((BR, SHELL, 128), jnp.bfloat16),
            pltpu.VMEM((SHELL, 512), jnp.bfloat16),
            pltpu.SemaphoreType.DMA((BR // 2 + 1,)),
            pltpu.SemaphoreType.DMA((SLOTS + 2,)),
        ],
        compiler_params=params(),
        name="pack_shells",
    )(send, feats, occ, pick)


def first_own(feats, occ, weights):
    return pl.pallas_call(
        first_own_kernel,
        grid=GRID,
        in_specs=[pair_spec(), WHOLE(), WHOLE()],
        out_specs=[part_spec(), pair_spec(), pair_spec(), shell_pair_spec()],
        out_shape=[PARTIAL, FIELD, FIELD] + shells_of(BR),
        scratch_shapes=own_scratch(),
        compiler_params=params(),
        cost_estimate=OWN_COST,
        name="first_own",
    )(feats, occ, weights)


def second_own(hidden, x, weights):
    return pl.pallas_call(
        second_own_kernel,
        grid=GRID,
        in_specs=[pair_spec(), pair_spec(), WHOLE()],
        out_specs=[part_spec(), shell_pair_spec()],
        out_shape=[PARTIAL] + shells_of(BR),
        scratch_shapes=own_scratch(),
        compiler_params=params(),
        cost_estimate=OWN_COST,
        name="second_own",
    )(hidden, x, weights)


def first_halo(src, send, pick, part, mask, weights, shells, near, far, recv):
    return pl.pallas_call(
        first_halo_kernel,
        in_specs=[SCALARS(), SCALARS(), WHOLE()] + [ANYWHERE()] * 7,
        out_specs=[ANYWHERE()] * 4,
        out_shape=[FIELD] + shells_of(SLOTS, EDGE, EDGE),
        scratch_shapes=halo_scratch() + own_shells_scratch(),
        compiler_params=params(),
        cost_estimate=HALO_COST,
        name="first_halo",
    )(src, send, pick, part, mask, weights, shells, near, far, recv)


def second_halo(src, part, mask, weights, shells, near, far, recv):
    return pl.pallas_call(
        second_halo_kernel,
        in_specs=[SCALARS()] + [ANYWHERE()] * 7,
        out_specs=ANYWHERE(),
        out_shape=FIELD,
        scratch_shapes=halo_scratch(),
        compiler_params=params(),
        cost_estimate=HALO_COST,
        name="second_halo",
    )(src, part, mask, weights, shells, near, far, recv)


def swapped(value, begin):
    axes = ("grp", "dev")
    routes = []
    for device in range(begin, lax.axis_size(axes) - 1, 2):
        routes += [(device, device + 1), (device + 1, device)]
    return lax.ppermute(value, axes, routes)


def exchange(outgoing, near, far):
    arrived = lax.all_to_all(outgoing, "dev", split_axis=0, concat_axis=0, tiled=True)
    return swapped(near, 0), swapped(far, 1), arrived


def per_device(features, occupancy, w_first, w_second, src_ref, send_list):
    send = send_list.reshape(SLOTS)
    pick = shell_matrix()
    outgoing, near, far = pack(send, features, occupancy, pick)
    pick = pick[FACE_LO:]
    around = exchange(outgoing, near, far)
    part, x, mask, shells = first_own(features, occupancy, w_first)
    hidden, outgoing, near, far = first_halo(src_ref, send, pick, part, mask, w_first, shells, *around)
    around = exchange(outgoing, near, far)
    part, shells = second_own(hidden, x, w_second)
    return second_halo(src_ref, part, mask, w_second, shells, *around)


def solution(mesh):
    placed = (
        P(("grp", "dev"), None, None),
        P(("grp", "dev"), None),
        P(),
        P(),
        P(("grp", "dev"), None),
        P(("grp", "dev"), None, None),
    )
    return jax.shard_map(
        per_device,
        mesh=mesh,
        in_specs=placed,
        out_specs=P(("grp", "dev"), None, None),
        check_vma=False,
    )
```

```python
import functools

import jax
import jax.numpy as jnp
import numpy as np
from jax import lax
from jax.experimental import pallas as pl
from jax.experimental.pallas import tpu as pltpu
from jax.sharding import PartitionSpec as P

BR = 12
EDGE = 2
SLOTS = 16
ENTRIES = BR + 2 * EDGE + SLOTS
BLANK = ENTRIES
SHELL = 304
FACE_LO = 224
FACE_HI = 260
MIB = 1024 * 1024
VMEM_LIMIT = 64 * MIB - 96 * 1024


def ring_row(x, y):
    if x == 0:
        return y * 8
    if x == 7:
        return 64 + y * 8
    if y == 0:
        return 128 + (x - 1) * 8
    if y == 7:
        return 176 + (x - 1) * 8
    return None


def cell_row(x, y, z):
    first = ring_row(x, y)
    if first is not None:
        return first + z
    return (FACE_LO if z == 0 else FACE_HI) + (x - 1) * 6 + (y - 1)


def shell_matrix():
    picked = np.zeros((SHELL, 512), np.float32)
    for x in range(8):
        for y in range(8):
            for z in range(8):
                cell = x * 64 + y * 8 + z
                first = ring_row(x, y)
                if first is not None:
                    picked[first + z, cell] = 1
                elif z in (0, 7):
                    picked[cell_row(x, y, z), cell] = 1
    return jnp.asarray(picked, jnp.bfloat16)


def store_shell(shell, planes):
    shell[0:64, :] = planes[0].astype(jnp.bfloat16)
    shell[64:128, :] = planes[7].astype(jnp.bfloat16)
    for x in (1, 3, 5):
        for start, rows in ((128, slice(0, 8)), (176, slice(56, 64))):
            both = jnp.concatenate([planes[x][rows], planes[x + 1][rows]], axis=0)
            shell[start + (x - 1) * 8 : start + (x + 1) * 8, :] = both.astype(jnp.bfloat16)


def store_inner(shell, planes, cells, inner):
    for x in range(1, 7):
        rows = (x - 1) * 6
        cells[x * 64 : x * 64 + 64, :] = planes[x]
        inner[rows : rows + 6, :] = cells[pl.ds(x * 64 + 8, 6, stride=8), :]
        inner[rows + 36 : rows + 42, :] = cells[pl.ds(x * 64 + 15, 6, stride=8), :]
    inner[72:80, :] = jnp.zeros((8, 128), jnp.float32)
    shell[FACE_LO:SHELL, :] = inner[...].astype(jnp.bfloat16)


def parity():
    return lax.rem(lax.axis_index("dev"), 2)


def start_all(copies):
    for copy in copies:
        copy.start()
    return copies


def wait_all(copies):
    for copy in copies:
        copy.wait()


def hand_out(send_ref, odd, own, out_ref, near_ref, far_ref, sems):
    first, second = jnp.where(odd == 0, BR - EDGE, 0), jnp.where(odd == 0, 0, BR - EDGE)
    copies = [pltpu.make_async_copy(own.at[pl.ds(first, EDGE)], near_ref, sems.at[SLOTS])]
    copies.append(pltpu.make_async_copy(own.at[pl.ds(second, EDGE)], far_ref, sems.at[SLOTS + 1]))
    for slot in range(SLOTS):
        brick = jnp.maximum(send_ref[slot], 0)
        copies.append(pltpu.make_async_copy(own.at[brick], out_ref.at[slot], sems.at[slot]))
    return start_all(copies)


def pack_kernel(
    send_ref, feat_ref, occ_ref, pick_ref, out_ref, near_ref, far_ref, feats, own, pick, in_sems, out_sems
):
    pick_load = pltpu.make_async_copy(pick_ref, pick, in_sems.at[BR // 2])
    pick_load.start()
    pairs = [pl.ds(pair * 2, 2) for pair in range(BR // 2)]
    loads = start_all(
        [pltpu.make_async_copy(feat_ref.at[at], feats.at[at], in_sems.at[n]) for n, at in enumerate(pairs)]
    )
    pick_load.wait()
    for part in range(0, BR // 2, 3):
        wait_all(loads[part : part + 3])
        for brick in range(2 * part, 2 * part + 6):
            held = occ_ref[brick : brick + 1, :].astype(jnp.float32).astype(jnp.bfloat16)
            chooser = pick[...] * jnp.broadcast_to(held, (SHELL, 512))
            shell = jnp.dot(chooser, feats[brick], preferred_element_type=jnp.float32)
            own[brick] = shell.astype(jnp.bfloat16)
    wait_all(hand_out(send_ref, parity(), own, out_ref, near_ref, far_ref, out_sems))


def toeplitz(target, taps):
    t0, t1, t2 = taps
    zero = jnp.zeros((128, 128), jnp.bfloat16)
    target[0, 0:128, 0:128] = t0
    target[0, 0:128, 128:256] = zero
    target[0, 128:256, 0:128] = t1
    target[0, 128:256, 128:256] = t0
    target[1, 0:128, 0:128] = t2
    target[1, 0:128, 128:256] = t1
    target[1, 128:256, 0:128] = zero
    target[1, 128:256, 128:256] = t2


def edge_masks():
    sub = lax.broadcasted_iota(jnp.int32, (8, 128), 0)
    return sub == 0, sub == 7


def shift_down(value, first, fill):
    return jnp.where(first, fill, pltpu.roll(value, 1, 0))


def shift_up(value, last, fill):
    return jnp.where(last, fill, pltpu.roll(value, 7, 0))


def own_pair(pair, plane, part_ref, wide, block, base):
    first, last = edge_masks()
    for x in range(8):
        planes = [plane(2 * pair + half, x) for half in range(2)]
        px = x + 1
        lanes = slice((px % 2) * 128, (px % 2) * 128 + 128)
        for y in range(8):
            mids = [planes[half][y * 8 : y * 8 + 8] for half in range(2)]
            for az, parts in enumerate(
                (
                    [shift_down(mid, first, 0.0) for mid in mids],
                    mids,
                    [shift_up(mid, last, 0.0) for mid in mids],
                )
            ):
                block[az, px // 2, y + 1, :, lanes] = jnp.concatenate(parts, axis=0).astype(jnp.bfloat16)
    acc = jnp.zeros((512, 256), jnp.float32)
    for az in range(3):
        for ay in range(3):
            for side in range(2):
                part = block[az, side : side + 4, ay : ay + 8].reshape(512, 256)
                acc = acc + jnp.dot(part, wide[ay * 3 + az, side], preferred_element_type=jnp.float32)
    if base is None:
        part_ref[pair] = acc
        return
    for half in range(2):
        for x in range(8):
            added = base(2 * pair + half, x)
            lanes = slice((x % 2) * 128, (x % 2) * 128 + 128)
            for y in range(8):
                row = (x // 2) * 128 + y * 16 + half * 8
                part_ref[pair, row : row + 8, lanes] = acc[row : row + 8, lanes] + added[y * 8 : y * 8 + 8]


def own_conv(plane, w_ref, part_ref, wide, block, base=None):
    step = pl.program_id(0)

    @pl.when(step == 0)
    def _():
        block[...] = jnp.zeros_like(block)
        for tap in range(9):
            toeplitz(wide.at[tap], (w_ref[tap], w_ref[9 + tap], w_ref[18 + tap]))

    for pair in range(STEP // 2):
        own_pair(pair, plane, part_ref, wide, block.at[pair], base)


def first_own_kernel(feat_ref, occ_ref, w_ref, part_ref, x_ref, mask_ref, shell_ref, wide, block, cells, inner):
    step = pl.program_id(0)
    rows = lax.broadcasted_iota(jnp.int32, (128, 128), 0)
    cols = lax.broadcasted_iota(jnp.int32, (128, 128), 1)
    diagonal = rows == cols
    ones = jnp.ones((128, 128), jnp.bfloat16)
    held = {}
    for half in range(STEP):
        occupied = occ_ref[pl.ds(step * STEP + half, 1), :].astype(jnp.float32)
        for chunk in range(4):
            at = slice(chunk * 128, chunk * 128 + 128)
            scale = jnp.where(diagonal, jnp.broadcast_to(occupied[:, at], (128, 128)), 0.0).astype(jnp.bfloat16)
            right = jnp.concatenate([feat_ref[half, at, :], ones], axis=1)
            both = jnp.dot(scale, right, preferred_element_type=jnp.float32)
            x_ref[half, at, :] = both[:, :128].astype(jnp.bfloat16)
            mask_ref[half, at, :] = both[:, 128:].astype(jnp.bfloat16)
            held[half, 2 * chunk] = both[:64, :128]
            held[half, 2 * chunk + 1] = both[64:, :128]
        planes = [held[half, x] for x in range(8)]
        store_shell(shell_ref.at[half], planes)
        store_inner(shell_ref.at[half], planes, cells.at[half], inner.at[half])
    own_conv(lambda half, x: held[half, x], w_ref, part_ref, wide, block)


def second_own_kernel(hidden_ref, x_ref, w_ref, part_ref, shell_ref, wide, block, cells, inner):
    plane = lambda ref: lambda half, x: ref[half, x * 64 : x * 64 + 64, :].astype(jnp.float32)
    for half in range(STEP):
        planes = [plane(hidden_ref)(half, x) for x in range(8)]
        store_shell(shell_ref.at[half], planes)
        store_inner(shell_ref.at[half], planes, cells.at[half], inner.at[half])
    own_conv(plane(hidden_ref), w_ref, part_ref, wide, block, plane(x_ref))


def fill_pool(pool, start, source):
    for entry in range(source.shape[0]):
        pool[start + entry] = source[entry].astype(jnp.float32)


def build_face(face, src_ref, pool, halo):
    first, last = edge_masks()
    delta, cell, z_cell = ((0, 7, 7), (2, 0, 0))[face % 2]

    def entry(brick, k):
        ref = src_ref[brick, k]
        return jnp.where(ref < 0, BLANK, ref)

    def put(pair, outer, parts):
        lanes = slice((outer % 2) * 128, (outer % 2) * 128 + 128)
        for shift in range(3):
            both = jnp.concatenate([parts[0][shift], parts[1][shift]], axis=0)
            halo[face, shift, outer // 2, pair * 16 : pair * 16 + 16, lanes] = both.astype(jnp.bfloat16)

    def column(around, x, y):
        below, here, above = around
        start, at_lo, at_hi = ring_row(x, y), cell_row(x, y, 7), cell_row(x, y, 0)
        mid = pool[here, start : start + 8, :]
        lo = jnp.broadcast_to(pool[below, at_lo : at_lo + 1, :], (8, 128))
        hi = jnp.broadcast_to(pool[above, at_hi : at_hi + 1, :], (8, 128))
        return shift_down(mid, first, lo), mid, shift_up(mid, last, hi)

    def z_plane(here, x):
        if x in (0, 7):
            mid = pool[here, pl.ds(ring_row(x, 0) + z_cell, 8, stride=8), :]
        else:
            start = cell_row(x, 1, z_cell) - 1
            at_lo, at_hi = cell_row(x, 0, z_cell), cell_row(x, 7, z_cell)
            mid = pool[here, start : start + 8, :]
            mid = jnp.where(first, jnp.broadcast_to(pool[here, at_lo : at_lo + 1, :], (8, 128)), mid)
            mid = jnp.where(last, jnp.broadcast_to(pool[here, at_hi : at_hi + 1, :], (8, 128)), mid)
        return shift_down(mid, first, 0.0), mid, shift_up(mid, last, 0.0)

    for pair in range(BR // 2):
        bricks = (2 * pair, 2 * pair + 1)
        if face < 2:
            around = [[[entry(b, delta * 9 + dy * 3 + dz) for dz in range(3)] for dy in range(3)] for b in bricks]
            for outer in range(10):
                dy = 0 if outer == 0 else (2 if outer == 9 else 1)
                y = 7 if outer == 0 else (0 if outer == 9 else outer - 1)
                put(pair, outer, [column(around[half][dy], cell, y) for half in range(2)])
        elif face < 4:
            around = [[entry(b, 9 + delta * 3 + dz) for dz in range(3)] for b in bricks]
            for x in range(8):
                put(pair, x + 1, [column(around[half], x, cell) for half in range(2)])
        else:
            here = [entry(b, 12 + delta) for b in bricks]
            for x in range(8):
                put(pair, x + 1, [z_plane(here[half], x) for half in range(2)])


def face_weights(face, w, along):
    end = 2 * (face % 2)
    for shift in range(3):
        taps = (
            [end * 9 + tap * 3 + shift for tap in range(3)],
            [tap * 9 + end * 3 + shift for tap in range(3)],
            [tap * 9 + shift * 3 + end for tap in range(3)],
        )[face // 2]
        toeplitz(along.at[face, shift], [w[tap] for tap in taps])


def sum_face(face, halo, along, sums):
    rows = 8 * BR
    acc = jnp.zeros((4 * rows, 256), jnp.float32)
    for shift in range(3):
        for side in range(2):
            part = halo[face, shift, side : side + 4].reshape(4 * rows, 256)
            acc = acc + jnp.dot(part, along[face, shift, side], preferred_element_type=jnp.float32)
    sums[face] = acc.reshape(4, BR, 8, 256)


def halo_part(odd, src_ref, sources, landed, sems, streams, stream_sems, pool, halo, along, sums):
    loads = start_all([pltpu.make_async_copy(a, b, sems.at[n]) for n, (a, b) in enumerate(zip(sources, landed))])
    pool[BLANK] = jnp.zeros((SHELL, 128), jnp.float32)
    for face in range(2, 6):
        for shift in range(3):
            halo[face, shift, 0, :, 0:128] = jnp.zeros((8 * BR, 128), jnp.bfloat16)
            halo[face, shift, 4, :, 128:256] = jnp.zeros((8 * BR, 128), jnp.bfloat16)
    near, far = BR + EDGE * (1 - odd), BR + EDGE * odd
    for load, start, field in zip(loads[:4], (0, near, far, BR + 2 * EDGE), landed[:4]):
        load.wait()
        if field is landed[3]:
            start_streams(streams, stream_sems)
        fill_pool(pool, start, field)

    build_face(0, src_ref, pool, halo)
    loads[4].wait()
    face_weights(0, landed[4], along)
    for face in range(6):
        if face < 5:
            build_face(face + 1, src_ref, pool, halo)
            face_weights(face + 1, landed[4], along)
        sum_face(face, halo, along, sums)


def start_streams(streams, stream_sems):
    for pair in range(BR // 2):
        for n, (source, target, size) in enumerate(streams):
            at = pl.ds(pair * size, size)
            pltpu.make_async_copy(source.at[at], target.at[at], stream_sems.at[n, pair]).start()


def wait_stream(streams, stream_sems, pair):
    for n, (source, target, size) in enumerate(streams):
        at = pl.ds(pair * size, size)
        pltpu.make_async_copy(source.at[at], target.at[at], stream_sems.at[n, pair]).wait()


def whole_plane(part, sums, pair, half, x):
    first, last = edge_masks()
    brick = pair * 2 + half
    lanes = slice((x % 2) * 128, (x % 2) * 128 + 128)
    columns = []
    for y in range(8):
        row = (x // 2) * 128 + y * 16 + half * 8
        value = part[pair, row : row + 8, lanes]
        if x in (0, 7):
            value = value + sums[x // 7, y // 2, brick, :, (y % 2) * 128 : (y % 2) * 128 + 128]
        if y in (0, 7):
            value = value + sums[2 + y // 7, x // 2, brick, :, lanes]
        lo = jnp.broadcast_to(sums[4, x // 2, brick, y : y + 1, lanes], (8, 128))
        hi = jnp.broadcast_to(sums[5, x // 2, brick, y : y + 1, lanes], (8, 128))
        columns.append(value + jnp.where(first, lo, jnp.where(last, hi, 0.0)))
    return jnp.concatenate(columns, axis=0)


def first_halo_kernel(
    src_ref, send_ref, pick_ref, part_ref, mask_ref, w_ref, shells_ref, near_in_ref, far_in_ref, recv_ref,
    hidden_ref, out_ref, near_ref, far_ref,
    pool, halo, along, sums, w, shells, near, far, recv, part, mask, done, sems, stream_sems, done_sems,
    own, out_sems, cells, inner,
):
    streams = ((part_ref, part, 1), (mask_ref, mask, 2))
    sources = (shells_ref, near_in_ref, far_in_ref, recv_ref, w_ref)
    landed = (shells, near, far, recv, w)
    halo_part(parity(), src_ref, sources, landed, sems, streams, stream_sems, pool, halo, along, sums)

    def store(pair):
        at = pl.ds(pair * 2, 2)
        return pltpu.make_async_copy(done.at[at], hidden_ref.at[at], done_sems.at[pair])

    def pair_body(pair, carry):
        wait_stream(streams, stream_sems, pair)
        for half in range(2):
            brick = pair * 2 + half
            planes = []
            for x in range(8):
                rows = slice(x * 64, x * 64 + 64)
                value = whole_plane(part, sums, pair, half, x)
                value = value / (1.0 + jnp.exp(-value)) * mask[brick, rows, :].astype(jnp.float32)
                done[brick, rows, :] = value.astype(jnp.bfloat16)
                planes.append(value)
            store_shell(own.at[brick], planes)
            store_inner(own.at[brick], planes, cells.at[half], inner.at[half])
        store(pair).start()
        return carry

    lax.fori_loop(0, BR // 2, pair_body, 0)
    copies = hand_out(send_ref, parity(), own, out_ref, near_ref, far_ref, out_sems)
    wait_all([store(pair) for pair in range(BR // 2)])
    wait_all(copies)


def second_halo_kernel(
    src_ref, part_ref, mask_ref, w_ref, shells_ref, near_in_ref, far_in_ref, recv_ref,
    result_ref,
    pool, halo, along, sums, w, shells, near, far, recv, part, mask, done, sems, stream_sems, done_sems,
):
    streams = ((part_ref, part, 1), (mask_ref, mask, 2))
    sources = (shells_ref, near_in_ref, far_in_ref, recv_ref, w_ref)
    landed = (shells, near, far, recv, w)
    halo_part(parity(), src_ref, sources, landed, sems, streams, stream_sems, pool, halo, along, sums)

    def store(pair):
        at = pl.ds(pair * 2, 2)
        return pltpu.make_async_copy(done.at[at], result_ref.at[at], done_sems.at[pair])

    def pair_body(pair, carry):
        wait_stream(streams, stream_sems, pair)
        for half in range(2):
            brick = pair * 2 + half
            for x in range(8):
                rows = slice(x * 64, x * 64 + 64)
                value = whole_plane(part, sums, pair, half, x)
                done[brick, rows, :] = (value * mask[brick, rows, :].astype(jnp.float32)).astype(jnp.bfloat16)
        store(pair).start()
        return carry

    lax.fori_loop(0, BR // 2, pair_body, 0)
    wait_all([store(pair) for pair in range(BR // 2)])


WHOLE = functools.partial(pl.BlockSpec, memory_space=pltpu.VMEM)
SCALARS = functools.partial(pl.BlockSpec, memory_space=pltpu.SMEM)
ANYWHERE = functools.partial(pl.BlockSpec, memory_space=pl.ANY)
STEP = 4
GRID = (BR // STEP,)
FIELD = jax.ShapeDtypeStruct((BR, 512, 128), jnp.bfloat16)
PARTIAL = jax.ShapeDtypeStruct((BR // 2, 512, 256), jnp.float32)


def pair_spec():
    return pl.BlockSpec((STEP, 512, 128), lambda i: (i, 0, 0))


def part_spec():
    return pl.BlockSpec((STEP // 2, 512, 256), lambda i: (i, 0, 0))


def shell_pair_spec():
    return pl.BlockSpec((STEP, SHELL, 128), lambda i: (i, 0, 0))


def shells_of(*counts):
    return [jax.ShapeDtypeStruct((n, SHELL, 128), jnp.bfloat16) for n in counts]


def params():
    return pltpu.CompilerParams(vmem_limit_bytes=VMEM_LIMIT)


def own_scratch():
    return [
        pltpu.VMEM((9, 2, 256, 256), jnp.bfloat16),
        pltpu.VMEM((STEP // 2, 3, 5, 10, 16, 256), jnp.bfloat16),
        pltpu.VMEM((STEP, 512, 128), jnp.float32),
        pltpu.VMEM((STEP, SHELL - FACE_LO, 128), jnp.float32),
    ]


def halo_scratch():
    shells = [pltpu.VMEM((n, SHELL, 128), jnp.bfloat16) for n in (BR, EDGE, EDGE, SLOTS)]
    return [
        pltpu.VMEM((ENTRIES + 1, SHELL, 128), jnp.float32),
        pltpu.VMEM((6, 3, 5, 8 * BR, 256), jnp.bfloat16),
        pltpu.VMEM((6, 3, 2, 256, 256), jnp.bfloat16),
        pltpu.VMEM((6, 4, BR, 8, 256), jnp.float32),
        pltpu.VMEM((27, 128, 128), jnp.bfloat16),
        *shells,
        pltpu.VMEM((BR // 2, 512, 256), jnp.float32),
        pltpu.VMEM((BR, 512, 128), jnp.bfloat16),
        pltpu.VMEM((BR, 512, 128), jnp.bfloat16),
        pltpu.SemaphoreType.DMA((5,)),
        pltpu.SemaphoreType.DMA((2, BR // 2)),
        pltpu.SemaphoreType.DMA((BR // 2,)),
    ]


def own_shells_scratch():
    return [pltpu.VMEM((BR, SHELL, 128), jnp.bfloat16), pltpu.SemaphoreType.DMA((SLOTS + 2,))]


OWN_COST = pl.CostEstimate(flops=2 * 6 * 512 * 4608 * 256, bytes_accessed=8 * MIB, transcendentals=0)
HALO_COST = pl.CostEstimate(flops=2 * 36 * 384 * 256 * 256, bytes_accessed=10 * MIB, transcendentals=0)


def pack(send, feats, occ, pick):
    return pl.pallas_call(
        pack_kernel,
        in_specs=[SCALARS(), ANYWHERE(), WHOLE(), ANYWHERE()],
        out_specs=[ANYWHERE()] * 3,
        out_shape=shells_of(SLOTS, EDGE, EDGE),
        scratch_shapes=[
            pltpu.VMEM((BR, 512, 128), jnp.bfloat16),
            pltpu.VMEM((BR, SHELL, 128), jnp.bfloat16),
            pltpu.VMEM((SHELL, 512), jnp.bfloat16),
            pltpu.SemaphoreType.DMA((BR // 2 + 1,)),
            pltpu.SemaphoreType.DMA((SLOTS + 2,)),
        ],
        compiler_params=params(),
        name="pack_shells",
    )(send, feats, occ, pick)


def first_own(feats, occ, weights):
    return pl.pallas_call(
        first_own_kernel,
        grid=GRID,
        in_specs=[pair_spec(), WHOLE(), WHOLE()],
        out_specs=[part_spec(), pair_spec(), pair_spec(), shell_pair_spec()],
        out_shape=[PARTIAL, FIELD, FIELD] + shells_of(BR),
        scratch_shapes=own_scratch(),
        compiler_params=params(),
        cost_estimate=OWN_COST,
        name="first_own",
    )(feats, occ, weights)


def second_own(hidden, x, weights):
    return pl.pallas_call(
        second_own_kernel,
        grid=GRID,
        in_specs=[pair_spec(), pair_spec(), WHOLE()],
        out_specs=[part_spec(), shell_pair_spec()],
        out_shape=[PARTIAL] + shells_of(BR),
        scratch_shapes=own_scratch(),
        compiler_params=params(),
        cost_estimate=OWN_COST,
        name="second_own",
    )(hidden, x, weights)


def first_halo(src, send, pick, part, mask, weights, shells, near, far, recv):
    return pl.pallas_call(
        first_halo_kernel,
        in_specs=[SCALARS(), SCALARS(), WHOLE()] + [ANYWHERE()] * 7,
        out_specs=[ANYWHERE()] * 4,
        out_shape=[FIELD] + shells_of(SLOTS, EDGE, EDGE),
        scratch_shapes=halo_scratch() + own_shells_scratch() + own_scratch()[2:],
        compiler_params=params(),
        cost_estimate=HALO_COST,
        name="first_halo",
    )(src, send, pick, part, mask, weights, shells, near, far, recv)


def second_halo(src, part, mask, weights, shells, near, far, recv):
    return pl.pallas_call(
        second_halo_kernel,
        in_specs=[SCALARS()] + [ANYWHERE()] * 7,
        out_specs=ANYWHERE(),
        out_shape=FIELD,
        scratch_shapes=halo_scratch(),
        compiler_params=params(),
        cost_estimate=HALO_COST,
        name="second_halo",
    )(src, part, mask, weights, shells, near, far, recv)


def swapped(value, begin):
    axes = ("grp", "dev")
    routes = []
    for device in range(begin, lax.axis_size(axes) - 1, 2):
        routes += [(device, device + 1), (device + 1, device)]
    return lax.ppermute(value, axes, routes)


def exchange(outgoing, near, far):
    arrived = lax.all_to_all(outgoing, "dev", split_axis=0, concat_axis=0, tiled=True)
    return swapped(near, 0), swapped(far, 1), arrived


def per_device(features, occupancy, w_first, w_second, src_ref, send_list):
    send = send_list.reshape(SLOTS)
    pick = shell_matrix()
    outgoing, near, far = pack(send, features, occupancy, pick)
    pick = pick[FACE_LO:]
    around = exchange(outgoing, near, far)
    part, x, mask, shells = first_own(features, occupancy, w_first)
    hidden, outgoing, near, far = first_halo(src_ref, send, pick, part, mask, w_first, shells, *around)
    around = exchange(outgoing, near, far)
    part, shells = second_own(hidden, x, w_second)
    return second_halo(src_ref, part, mask, w_second, shells, *around)


def solution(mesh):
    placed = (
        P(("grp", "dev"), None, None),
        P(("grp", "dev"), None),
        P(),
        P(),
        P(("grp", "dev"), None),
        P(("grp", "dev"), None, None),
    )
    return jax.shard_map(
        per_device,
        mesh=mesh,
        in_specs=placed,
        out_specs=P(("grp", "dev"), None, None),
        check_vma=False,
    )
```

```python
import functools

import jax
import jax.numpy as jnp
import numpy as np
from jax import lax
from jax.experimental import pallas as pl
from jax.experimental.pallas import tpu as pltpu
from jax.sharding import PartitionSpec as P

BR = 12
EDGE = 2
SLOTS = 16
ENTRIES = BR + 2 * EDGE + SLOTS
BLANK = ENTRIES
SHELL = 304
FACE_LO = 224
FACE_HI = 260
MIB = 1024 * 1024
VMEM_LIMIT = 64 * MIB - 96 * 1024


def ring_row(x, y):
    if x == 0:
        return y * 8
    if x == 7:
        return 64 + y * 8
    if y == 0:
        return 128 + (x - 1) * 8
    if y == 7:
        return 176 + (x - 1) * 8
    return None


def cell_row(x, y, z):
    first = ring_row(x, y)
    if first is not None:
        return first + z
    return (FACE_LO if z == 0 else FACE_HI) + (x - 1) * 6 + (y - 1)


def shell_matrix():
    picked = np.zeros((SHELL, 512), np.float32)
    for x in range(8):
        for y in range(8):
            for z in range(8):
                cell = x * 64 + y * 8 + z
                first = ring_row(x, y)
                if first is not None:
                    picked[first + z, cell] = 1
                elif z in (0, 7):
                    picked[cell_row(x, y, z), cell] = 1
    return jnp.asarray(picked, jnp.bfloat16)


def store_shell(shell, planes):
    shell[0:64, :] = planes[0].astype(jnp.bfloat16)
    shell[64:128, :] = planes[7].astype(jnp.bfloat16)
    for x in (1, 3, 5):
        for start, rows in ((128, slice(0, 8)), (176, slice(56, 64))):
            both = jnp.concatenate([planes[x][rows], planes[x + 1][rows]], axis=0)
            shell[start + (x - 1) * 8 : start + (x + 1) * 8, :] = both.astype(jnp.bfloat16)


def store_inner(shell, planes, cells, inner):
    for x in range(1, 7):
        rows = (x - 1) * 6
        cells[x * 64 : x * 64 + 64, :] = planes[x]
        inner[rows : rows + 6, :] = cells[pl.ds(x * 64 + 8, 6, stride=8), :]
        inner[rows + 36 : rows + 42, :] = cells[pl.ds(x * 64 + 15, 6, stride=8), :]
    inner[72:80, :] = jnp.zeros((8, 128), jnp.float32)
    shell[FACE_LO:SHELL, :] = inner[...].astype(jnp.bfloat16)


def parity():
    return lax.rem(lax.axis_index("dev"), 2)


def start_all(copies):
    for copy in copies:
        copy.start()
    return copies


def wait_all(copies):
    for copy in copies:
        copy.wait()


def send_below(send_ref, own, out_ref, sems, begin, end):
    for slot in range(SLOTS):
        brick = jnp.maximum(send_ref[slot], 0)

        @pl.when((brick >= begin) & (brick < end))
        def _():
            pltpu.make_async_copy(own.at[brick], out_ref.at[slot], sems.at[slot]).start()


def hand_out(send_ref, odd, own, out_ref, near_ref, far_ref, sems, slots_too=True):
    first, second = jnp.where(odd == 0, BR - EDGE, 0), jnp.where(odd == 0, 0, BR - EDGE)
    copies = [pltpu.make_async_copy(own.at[pl.ds(first, EDGE)], near_ref, sems.at[SLOTS])]
    copies.append(pltpu.make_async_copy(own.at[pl.ds(second, EDGE)], far_ref, sems.at[SLOTS + 1]))
    start_all(copies)
    for slot in range(SLOTS):
        brick = jnp.maximum(send_ref[slot], 0)
        copies.append(pltpu.make_async_copy(own.at[brick], out_ref.at[slot], sems.at[slot]))
        if slots_too:
            copies[-1].start()
    return copies


def pack_kernel(
    send_ref, feat_ref, occ_ref, pick_ref, out_ref, near_ref, far_ref, feats, own, pick, in_sems, out_sems
):
    pick_load = pltpu.make_async_copy(pick_ref, pick, in_sems.at[BR // 2])
    pick_load.start()
    pairs = [pl.ds(pair * 2, 2) for pair in range(BR // 2)]
    loads = start_all(
        [pltpu.make_async_copy(feat_ref.at[at], feats.at[at], in_sems.at[n]) for n, at in enumerate(pairs)]
    )
    pick_load.wait()
    for part in range(0, BR // 2, 3):
        wait_all(loads[part : part + 3])
        for brick in range(2 * part, 2 * part + 6):
            held = occ_ref[brick : brick + 1, :].astype(jnp.float32).astype(jnp.bfloat16)
            chooser = pick[...] * jnp.broadcast_to(held, (SHELL, 512))
            shell = jnp.dot(chooser, feats[brick], preferred_element_type=jnp.float32)
            own[brick] = shell.astype(jnp.bfloat16)
        send_below(send_ref, own, out_ref, out_sems, 2 * part, 2 * part + 6)
    wait_all(hand_out(send_ref, parity(), own, out_ref, near_ref, far_ref, out_sems, False))


def toeplitz(target, taps):
    t0, t1, t2 = taps
    zero = jnp.zeros((128, 128), jnp.bfloat16)
    target[0, 0:128, 0:128] = t0
    target[0, 0:128, 128:256] = zero
    target[0, 128:256, 0:128] = t1
    target[0, 128:256, 128:256] = t0
    target[1, 0:128, 0:128] = t2
    target[1, 0:128, 128:256] = t1
    target[1, 128:256, 0:128] = zero
    target[1, 128:256, 128:256] = t2


def edge_masks():
    sub = lax.broadcasted_iota(jnp.int32, (8, 128), 0)
    return sub == 0, sub == 7


def shift_down(value, first, fill):
    return jnp.where(first, fill, pltpu.roll(value, 1, 0))


def shift_up(value, last, fill):
    return jnp.where(last, fill, pltpu.roll(value, 7, 0))


def own_pair(pair, plane, part_ref, wide, block, base):
    first, last = edge_masks()
    for x in range(8):
        planes = [plane(2 * pair + half, x) for half in range(2)]
        px = x + 1
        lanes = slice((px % 2) * 128, (px % 2) * 128 + 128)
        for y in range(8):
            mids = [planes[half][y * 8 : y * 8 + 8] for half in range(2)]
            for az, parts in enumerate(
                (
                    [shift_down(mid, first, 0.0) for mid in mids],
                    mids,
                    [shift_up(mid, last, 0.0) for mid in mids],
                )
            ):
                block[az, px // 2, y + 1, :, lanes] = jnp.concatenate(parts, axis=0).astype(jnp.bfloat16)
    acc = jnp.zeros((512, 256), jnp.float32)
    for az in range(3):
        for ay in range(3):
            for side in range(2):
                part = block[az, side : side + 4, ay : ay + 8].reshape(512, 256)
                acc = acc + jnp.dot(part, wide[ay * 3 + az, side], preferred_element_type=jnp.float32)
    if base is None:
        part_ref[pair] = acc
        return
    for half in range(2):
        for x in range(8):
            added = base(2 * pair + half, x)
            lanes = slice((x % 2) * 128, (x % 2) * 128 + 128)
            for y in range(8):
                row = (x // 2) * 128 + y * 16 + half * 8
                part_ref[pair, row : row + 8, lanes] = acc[row : row + 8, lanes] + added[y * 8 : y * 8 + 8]


def own_conv(plane, w_ref, part_ref, wide, block, base=None):
    step = pl.program_id(0)

    @pl.when(step == 0)
    def _():
        block[...] = jnp.zeros_like(block)
        for tap in range(9):
            toeplitz(wide.at[tap], (w_ref[tap], w_ref[9 + tap], w_ref[18 + tap]))

    for pair in range(STEP // 2):
        own_pair(pair, plane, part_ref, wide, block.at[pair], base)


def first_own_kernel(feat_ref, occ_ref, w_ref, part_ref, x_ref, mask_ref, shell_ref, wide, block, cells, inner):
    step = pl.program_id(0)
    rows = lax.broadcasted_iota(jnp.int32, (128, 128), 0)
    cols = lax.broadcasted_iota(jnp.int32, (128, 128), 1)
    diagonal = rows == cols
    ones = jnp.ones((128, 128), jnp.bfloat16)
    held = {}
    for half in range(STEP):
        occupied = occ_ref[pl.ds(step * STEP + half, 1), :].astype(jnp.float32)
        for chunk in range(4):
            at = slice(chunk * 128, chunk * 128 + 128)
            scale = jnp.where(diagonal, jnp.broadcast_to(occupied[:, at], (128, 128)), 0.0).astype(jnp.bfloat16)
            right = jnp.concatenate([feat_ref[half, at, :], ones], axis=1)
            both = jnp.dot(scale, right, preferred_element_type=jnp.float32)
            x_ref[half, at, :] = both[:, :128].astype(jnp.bfloat16)
            mask_ref[half, at, :] = both[:, 128:].astype(jnp.bfloat16)
            held[half, 2 * chunk] = both[:64, :128]
            held[half, 2 * chunk + 1] = both[64:, :128]
        planes = [held[half, x] for x in range(8)]
        store_shell(shell_ref.at[half], planes)
        store_inner(shell_ref.at[half], planes, cells.at[half], inner.at[half])
    own_conv(lambda half, x: held[half, x], w_ref, part_ref, wide, block)


def second_own_kernel(hidden_ref, x_ref, w_ref, part_ref, shell_ref, wide, block, cells, inner):
    plane = lambda ref: lambda half, x: ref[half, x * 64 : x * 64 + 64, :].astype(jnp.float32)
    for half in range(STEP):
        planes = [plane(hidden_ref)(half, x) for x in range(8)]
        store_shell(shell_ref.at[half], planes)
        store_inner(shell_ref.at[half], planes, cells.at[half], inner.at[half])
    own_conv(plane(hidden_ref), w_ref, part_ref, wide, block, plane(x_ref))


def fill_pool(pool, start, source):
    for entry in range(source.shape[0]):
        pool[start + entry] = source[entry].astype(jnp.float32)


def build_face(face, src_ref, pool, halo):
    first, last = edge_masks()
    delta, cell, z_cell = ((0, 7, 7), (2, 0, 0))[face % 2]

    def entry(brick, k):
        ref = src_ref[brick, k]
        return jnp.where(ref < 0, BLANK, ref)

    def put(pair, outer, parts):
        lanes = slice((outer % 2) * 128, (outer % 2) * 128 + 128)
        for shift in range(3):
            both = jnp.concatenate([parts[0][shift], parts[1][shift]], axis=0)
            halo[face, shift, outer // 2, pair * 16 : pair * 16 + 16, lanes] = both.astype(jnp.bfloat16)

    def column(around, x, y):
        below, here, above = around
        start, at_lo, at_hi = ring_row(x, y), cell_row(x, y, 7), cell_row(x, y, 0)
        mid = pool[here, start : start + 8, :]
        lo = jnp.broadcast_to(pool[below, at_lo : at_lo + 1, :], (8, 128))
        hi = jnp.broadcast_to(pool[above, at_hi : at_hi + 1, :], (8, 128))
        return shift_down(mid, first, lo), mid, shift_up(mid, last, hi)

    def z_plane(here, x):
        if x in (0, 7):
            mid = pool[here, pl.ds(ring_row(x, 0) + z_cell, 8, stride=8), :]
        else:
            start = cell_row(x, 1, z_cell) - 1
            at_lo, at_hi = cell_row(x, 0, z_cell), cell_row(x, 7, z_cell)
            mid = pool[here, start : start + 8, :]
            mid = jnp.where(first, jnp.broadcast_to(pool[here, at_lo : at_lo + 1, :], (8, 128)), mid)
            mid = jnp.where(last, jnp.broadcast_to(pool[here, at_hi : at_hi + 1, :], (8, 128)), mid)
        return shift_down(mid, first, 0.0), mid, shift_up(mid, last, 0.0)

    for pair in range(BR // 2):
        bricks = (2 * pair, 2 * pair + 1)
        if face < 2:
            around = [[[entry(b, delta * 9 + dy * 3 + dz) for dz in range(3)] for dy in range(3)] for b in bricks]
            for outer in range(10):
                dy = 0 if outer == 0 else (2 if outer == 9 else 1)
                y = 7 if outer == 0 else (0 if outer == 9 else outer - 1)
                put(pair, outer, [column(around[half][dy], cell, y) for half in range(2)])
        elif face < 4:
            around = [[entry(b, 9 + delta * 3 + dz) for dz in range(3)] for b in bricks]
            for x in range(8):
                put(pair, x + 1, [column(around[half], x, cell) for half in range(2)])
        else:
            here = [entry(b, 12 + delta) for b in bricks]
            for x in range(8):
                put(pair, x + 1, [z_plane(here[half], x) for half in range(2)])


def face_weights(face, w, along):
    end = 2 * (face % 2)
    for shift in range(3):
        taps = (
            [end * 9 + tap * 3 + shift for tap in range(3)],
            [tap * 9 + end * 3 + shift for tap in range(3)],
            [tap * 9 + shift * 3 + end for tap in range(3)],
        )[face // 2]
        toeplitz(along.at[face, shift], [w[tap] for tap in taps])


def sum_face(face, halo, along, sums):
    rows = 8 * BR
    acc = jnp.zeros((4 * rows, 256), jnp.float32)
    for shift in range(3):
        for side in range(2):
            part = halo[face, shift, side : side + 4].reshape(4 * rows, 256)
            acc = acc + jnp.dot(part, along[face, shift, side], preferred_element_type=jnp.float32)
    sums[face] = acc.reshape(4, BR, 8, 256)


def halo_part(odd, src_ref, sources, landed, sems, streams, stream_sems, pool, halo, along, sums):
    loads = start_all([pltpu.make_async_copy(a, b, sems.at[n]) for n, (a, b) in enumerate(zip(sources, landed))])
    pool[BLANK] = jnp.zeros((SHELL, 128), jnp.float32)
    for face in range(2, 6):
        for shift in range(3):
            halo[face, shift, 0, :, 0:128] = jnp.zeros((8 * BR, 128), jnp.bfloat16)
            halo[face, shift, 4, :, 128:256] = jnp.zeros((8 * BR, 128), jnp.bfloat16)
    near, far = BR + EDGE * (1 - odd), BR + EDGE * odd
    for load, start, field in zip(loads[:4], (0, near, far, BR + 2 * EDGE), landed[:4]):
        load.wait()
        if field is landed[3]:
            start_streams(streams, stream_sems)
        fill_pool(pool, start, field)

    build_face(0, src_ref, pool, halo)
    loads[4].wait()
    face_weights(0, landed[4], along)
    for face in range(6):
        if face < 5:
            build_face(face + 1, src_ref, pool, halo)
            face_weights(face + 1, landed[4], along)
        sum_face(face, halo, along, sums)


def start_streams(streams, stream_sems):
    for pair in range(BR // 2):
        for n, (source, target, size) in enumerate(streams):
            at = pl.ds(pair * size, size)
            pltpu.make_async_copy(source.at[at], target.at[at], stream_sems.at[n, pair]).start()


def wait_stream(streams, stream_sems, pair):
    for n, (source, target, size) in enumerate(streams):
        at = pl.ds(pair * size, size)
        pltpu.make_async_copy(source.at[at], target.at[at], stream_sems.at[n, pair]).wait()


def whole_plane(part, sums, pair, half, x):
    first, last = edge_masks()
    brick = pair * 2 + half
    lanes = slice((x % 2) * 128, (x % 2) * 128 + 128)
    columns = []
    for y in range(8):
        row = (x // 2) * 128 + y * 16 + half * 8
        value = part[pair, row : row + 8, lanes]
        if x in (0, 7):
            value = value + sums[x // 7, y // 2, brick, :, (y % 2) * 128 : (y % 2) * 128 + 128]
        if y in (0, 7):
            value = value + sums[2 + y // 7, x // 2, brick, :, lanes]
        lo = jnp.broadcast_to(sums[4, x // 2, brick, y : y + 1, lanes], (8, 128))
        hi = jnp.broadcast_to(sums[5, x // 2, brick, y : y + 1, lanes], (8, 128))
        columns.append(value + jnp.where(first, lo, jnp.where(last, hi, 0.0)))
    return jnp.concatenate(columns, axis=0)


def first_halo_kernel(
    src_ref, send_ref, pick_ref, part_ref, mask_ref, w_ref, shells_ref, near_in_ref, far_in_ref, recv_ref,
    hidden_ref, out_ref, near_ref, far_ref,
    pool, halo, along, sums, w, shells, near, far, recv, part, mask, done, sems, stream_sems, done_sems,
    own, out_sems, cells, inner,
):
    streams = ((part_ref, part, 1), (mask_ref, mask, 2))
    sources = (shells_ref, near_in_ref, far_in_ref, recv_ref, w_ref)
    landed = (shells, near, far, recv, w)
    halo_part(parity(), src_ref, sources, landed, sems, streams, stream_sems, pool, halo, along, sums)

    def store(pair):
        at = pl.ds(pair * 2, 2)
        return pltpu.make_async_copy(done.at[at], hidden_ref.at[at], done_sems.at[pair])

    def pair_body(pair, carry):
        wait_stream(streams, stream_sems, pair)
        for half in range(2):
            brick = pair * 2 + half
            planes = []
            for x in range(8):
                rows = slice(x * 64, x * 64 + 64)
                value = whole_plane(part, sums, pair, half, x)
                value = value / (1.0 + jnp.exp(-value)) * mask[brick, rows, :].astype(jnp.float32)
                done[brick, rows, :] = value.astype(jnp.bfloat16)
                planes.append(value)
            store_shell(own.at[brick], planes)
            store_inner(own.at[brick], planes, cells.at[half], inner.at[half])
        store(pair).start()
        return carry

    lax.fori_loop(0, BR // 4, pair_body, 0)
    send_below(send_ref, own, out_ref, out_sems, 0, BR // 2)
    lax.fori_loop(BR // 4, BR // 2, pair_body, 0)
    send_below(send_ref, own, out_ref, out_sems, BR // 2, BR)
    copies = hand_out(send_ref, parity(), own, out_ref, near_ref, far_ref, out_sems, False)
    wait_all([store(pair) for pair in range(BR // 2)])
    wait_all(copies)


def second_halo_kernel(
    src_ref, part_ref, mask_ref, w_ref, shells_ref, near_in_ref, far_in_ref, recv_ref,
    result_ref,
    pool, halo, along, sums, w, shells, near, far, recv, part, mask, done, sems, stream_sems, done_sems,
):
    streams = ((part_ref, part, 1), (mask_ref, mask, 2))
    sources = (shells_ref, near_in_ref, far_in_ref, recv_ref, w_ref)
    landed = (shells, near, far, recv, w)
    halo_part(parity(), src_ref, sources, landed, sems, streams, stream_sems, pool, halo, along, sums)

    def store(pair):
        at = pl.ds(pair * 2, 2)
        return pltpu.make_async_copy(done.at[at], result_ref.at[at], done_sems.at[pair])

    def pair_body(pair, carry):
        wait_stream(streams, stream_sems, pair)
        for half in range(2):
            brick = pair * 2 + half
            for x in range(8):
                rows = slice(x * 64, x * 64 + 64)
                value = whole_plane(part, sums, pair, half, x)
                done[brick, rows, :] = (value * mask[brick, rows, :].astype(jnp.float32)).astype(jnp.bfloat16)
        store(pair).start()
        return carry

    lax.fori_loop(0, BR // 2, pair_body, 0)
    wait_all([store(pair) for pair in range(BR // 2)])


WHOLE = functools.partial(pl.BlockSpec, memory_space=pltpu.VMEM)
SCALARS = functools.partial(pl.BlockSpec, memory_space=pltpu.SMEM)
ANYWHERE = functools.partial(pl.BlockSpec, memory_space=pl.ANY)
STEP = 4
GRID = (BR // STEP,)
FIELD = jax.ShapeDtypeStruct((BR, 512, 128), jnp.bfloat16)
PARTIAL = jax.ShapeDtypeStruct((BR // 2, 512, 256), jnp.float32)


def pair_spec():
    return pl.BlockSpec((STEP, 512, 128), lambda i: (i, 0, 0))


def part_spec():
    return pl.BlockSpec((STEP // 2, 512, 256), lambda i: (i, 0, 0))


def shell_pair_spec():
    return pl.BlockSpec((STEP, SHELL, 128), lambda i: (i, 0, 0))


def shells_of(*counts):
    return [jax.ShapeDtypeStruct((n, SHELL, 128), jnp.bfloat16) for n in counts]


def params():
    return pltpu.CompilerParams(vmem_limit_bytes=VMEM_LIMIT)


def own_scratch():
    return [
        pltpu.VMEM((9, 2, 256, 256), jnp.bfloat16),
        pltpu.VMEM((STEP // 2, 3, 5, 10, 16, 256), jnp.bfloat16),
        pltpu.VMEM((STEP, 512, 128), jnp.float32),
        pltpu.VMEM((STEP, SHELL - FACE_LO, 128), jnp.float32),
    ]


def halo_scratch():
    shells = [pltpu.VMEM((n, SHELL, 128), jnp.bfloat16) for n in (BR, EDGE, EDGE, SLOTS)]
    return [
        pltpu.VMEM((ENTRIES + 1, SHELL, 128), jnp.float32),
        pltpu.VMEM((6, 3, 5, 8 * BR, 256), jnp.bfloat16),
        pltpu.VMEM((6, 3, 2, 256, 256), jnp.bfloat16),
        pltpu.VMEM((6, 4, BR, 8, 256), jnp.float32),
        pltpu.VMEM((27, 128, 128), jnp.bfloat16),
        *shells,
        pltpu.VMEM((BR // 2, 512, 256), jnp.float32),
        pltpu.VMEM((BR, 512, 128), jnp.bfloat16),
        pltpu.VMEM((BR, 512, 128), jnp.bfloat16),
        pltpu.SemaphoreType.DMA((5,)),
        pltpu.SemaphoreType.DMA((2, BR // 2)),
        pltpu.SemaphoreType.DMA((BR // 2,)),
    ]


def own_shells_scratch():
    return [pltpu.VMEM((BR, SHELL, 128), jnp.bfloat16), pltpu.SemaphoreType.DMA((SLOTS + 2,))]


OWN_COST = pl.CostEstimate(flops=2 * 6 * 512 * 4608 * 256, bytes_accessed=8 * MIB, transcendentals=0)
HALO_COST = pl.CostEstimate(flops=2 * 36 * 384 * 256 * 256, bytes_accessed=10 * MIB, transcendentals=0)


def pack(send, feats, occ, pick):
    return pl.pallas_call(
        pack_kernel,
        in_specs=[SCALARS(), ANYWHERE(), WHOLE(), ANYWHERE()],
        out_specs=[ANYWHERE()] * 3,
        out_shape=shells_of(SLOTS, EDGE, EDGE),
        scratch_shapes=[
            pltpu.VMEM((BR, 512, 128), jnp.bfloat16),
            pltpu.VMEM((BR, SHELL, 128), jnp.bfloat16),
            pltpu.VMEM((SHELL, 512), jnp.bfloat16),
            pltpu.SemaphoreType.DMA((BR // 2 + 1,)),
            pltpu.SemaphoreType.DMA((SLOTS + 2,)),
        ],
        compiler_params=params(),
        name="pack_shells",
    )(send, feats, occ, pick)


def first_own(feats, occ, weights):
    return pl.pallas_call(
        first_own_kernel,
        grid=GRID,
        in_specs=[pair_spec(), WHOLE(), WHOLE()],
        out_specs=[part_spec(), pair_spec(), pair_spec(), shell_pair_spec()],
        out_shape=[PARTIAL, FIELD, FIELD] + shells_of(BR),
        scratch_shapes=own_scratch(),
        compiler_params=params(),
        cost_estimate=OWN_COST,
        name="first_own",
    )(feats, occ, weights)


def second_own(hidden, x, weights):
    return pl.pallas_call(
        second_own_kernel,
        grid=GRID,
        in_specs=[pair_spec(), pair_spec(), WHOLE()],
        out_specs=[part_spec(), shell_pair_spec()],
        out_shape=[PARTIAL] + shells_of(BR),
        scratch_shapes=own_scratch(),
        compiler_params=params(),
        cost_estimate=OWN_COST,
        name="second_own",
    )(hidden, x, weights)


def first_halo(src, send, pick, part, mask, weights, shells, near, far, recv):
    return pl.pallas_call(
        first_halo_kernel,
        in_specs=[SCALARS(), SCALARS(), WHOLE()] + [ANYWHERE()] * 7,
        out_specs=[ANYWHERE()] * 4,
        out_shape=[FIELD] + shells_of(SLOTS, EDGE, EDGE),
        scratch_shapes=halo_scratch() + own_shells_scratch() + own_scratch()[2:],
        compiler_params=params(),
        cost_estimate=HALO_COST,
        name="first_halo",
    )(src, send, pick, part, mask, weights, shells, near, far, recv)


def second_halo(src, part, mask, weights, shells, near, far, recv):
    return pl.pallas_call(
        second_halo_kernel,
        in_specs=[SCALARS()] + [ANYWHERE()] * 7,
        out_specs=ANYWHERE(),
        out_shape=FIELD,
        scratch_shapes=halo_scratch(),
        compiler_params=params(),
        cost_estimate=HALO_COST,
        name="second_halo",
    )(src, part, mask, weights, shells, near, far, recv)


def swapped(value, begin):
    axes = ("grp", "dev")
    routes = []
    for device in range(begin, lax.axis_size(axes) - 1, 2):
        routes += [(device, device + 1), (device + 1, device)]
    return lax.ppermute(value, axes, routes)


def exchange(outgoing, near, far):
    arrived = lax.all_to_all(outgoing, "dev", split_axis=0, concat_axis=0, tiled=True)
    return swapped(near, 0), swapped(far, 1), arrived


def per_device(features, occupancy, w_first, w_second, src_ref, send_list):
    send = send_list.reshape(SLOTS)
    pick = shell_matrix()
    outgoing, near, far = pack(send, features, occupancy, pick)
    pick = pick[FACE_LO:]
    around = exchange(outgoing, near, far)
    part, x, mask, shells = first_own(features, occupancy, w_first)
    hidden, outgoing, near, far = first_halo(src_ref, send, pick, part, mask, w_first, shells, *around)
    around = exchange(outgoing, near, far)
    part, shells = second_own(hidden, x, w_second)
    return second_halo(src_ref, part, mask, w_second, shells, *around)


def solution(mesh):
    placed = (
        P(("grp", "dev"), None, None),
        P(("grp", "dev"), None),
        P(),
        P(),
        P(("grp", "dev"), None),
        P(("grp", "dev"), None, None),
    )
    return jax.shard_map(
        per_device,
        mesh=mesh,
        in_specs=placed,
        out_specs=P(("grp", "dev"), None, None),
        check_vma=False,
    )
```

```python
import functools

import jax
import jax.numpy as jnp
import numpy as np
from jax import lax
from jax.experimental import pallas as pl
from jax.experimental.pallas import tpu as pltpu
from jax.sharding import PartitionSpec as P

BR = 12
EDGE = 2
SLOTS = 16
ENTRIES = BR + 2 * EDGE + SLOTS
BLANK = ENTRIES
SHELL = 304
FACE_LO = 224
FACE_HI = 260
MIB = 1024 * 1024
VMEM_LIMIT = 64 * MIB - 96 * 1024


def ring_row(x, y):
    if x == 0:
        return y * 8
    if x == 7:
        return 64 + y * 8
    if y == 0:
        return 128 + (x - 1) * 8
    if y == 7:
        return 176 + (x - 1) * 8
    return None


def cell_row(x, y, z):
    first = ring_row(x, y)
    if first is not None:
        return first + z
    return (FACE_LO if z == 0 else FACE_HI) + (x - 1) * 6 + (y - 1)


def shell_matrix():
    picked = np.zeros((SHELL, 512), np.float32)
    for x in range(8):
        for y in range(8):
            for z in range(8):
                cell = x * 64 + y * 8 + z
                first = ring_row(x, y)
                if first is not None:
                    picked[first + z, cell] = 1
                elif z in (0, 7):
                    picked[cell_row(x, y, z), cell] = 1
    return jnp.asarray(picked, jnp.bfloat16)


def store_shell(shell, planes):
    shell[0:64, :] = planes[0].astype(jnp.bfloat16)
    shell[64:128, :] = planes[7].astype(jnp.bfloat16)
    for x in (1, 3, 5):
        for start, rows in ((128, slice(0, 8)), (176, slice(56, 64))):
            both = jnp.concatenate([planes[x][rows], planes[x + 1][rows]], axis=0)
            shell[start + (x - 1) * 8 : start + (x + 1) * 8, :] = both.astype(jnp.bfloat16)


def store_inner(shell, planes, cells, inner):
    for x in range(1, 7):
        rows = (x - 1) * 6
        cells[x * 64 : x * 64 + 64, :] = planes[x]
        inner[rows : rows + 6, :] = cells[pl.ds(x * 64 + 8, 6, stride=8), :]
        inner[rows + 36 : rows + 42, :] = cells[pl.ds(x * 64 + 15, 6, stride=8), :]
    inner[72:80, :] = jnp.zeros((8, 128), jnp.float32)
    shell[FACE_LO:SHELL, :] = inner[...].astype(jnp.bfloat16)


def parity():
    return lax.rem(lax.axis_index("dev"), 2)


def start_all(copies):
    for copy in copies:
        copy.start()
    return copies


def wait_all(copies):
    for copy in copies:
        copy.wait()


def send_below(send_ref, own, out_ref, sems, begin, end):
    for slot in range(SLOTS):
        brick = jnp.maximum(send_ref[slot], 0)

        @pl.when((brick >= begin) & (brick < end))
        def _():
            pltpu.make_async_copy(own.at[brick], out_ref.at[slot], sems.at[slot]).start()


def hand_out(send_ref, odd, own, out_ref, near_ref, far_ref, sems, slots_too=True):
    first, second = jnp.where(odd == 0, BR - EDGE, 0), jnp.where(odd == 0, 0, BR - EDGE)
    copies = [pltpu.make_async_copy(own.at[pl.ds(first, EDGE)], near_ref, sems.at[SLOTS])]
    copies.append(pltpu.make_async_copy(own.at[pl.ds(second, EDGE)], far_ref, sems.at[SLOTS + 1]))
    start_all(copies)
    for slot in range(SLOTS):
        brick = jnp.maximum(send_ref[slot], 0)
        copies.append(pltpu.make_async_copy(own.at[brick], out_ref.at[slot], sems.at[slot]))
        if slots_too:
            copies[-1].start()
    return copies


def pack_kernel(
    send_ref, feat_ref, occ_ref, pick_ref, out_ref, near_ref, far_ref, feats, own, pick, in_sems, out_sems
):
    pick_load = pltpu.make_async_copy(pick_ref, pick, in_sems.at[BR // 2])
    pick_load.start()
    pairs = [pl.ds(pair * 2, 2) for pair in range(BR // 2)]
    loads = start_all(
        [pltpu.make_async_copy(feat_ref.at[at], feats.at[at], in_sems.at[n]) for n, at in enumerate(pairs)]
    )
    pick_load.wait()
    for part in range(0, BR // 2, 3):
        wait_all(loads[part : part + 3])
        for brick in range(2 * part, 2 * part + 6):
            held = occ_ref[brick : brick + 1, :].astype(jnp.float32).astype(jnp.bfloat16)
            chooser = pick[...] * jnp.broadcast_to(held, (SHELL, 512))
            shell = jnp.dot(chooser, feats[brick], preferred_element_type=jnp.float32)
            own[brick] = shell.astype(jnp.bfloat16)
        send_below(send_ref, own, out_ref, out_sems, 2 * part, 2 * part + 6)
    wait_all(hand_out(send_ref, parity(), own, out_ref, near_ref, far_ref, out_sems, False))


def toeplitz(target, taps):
    t0, t1, t2 = taps
    zero = jnp.zeros((128, 128), jnp.bfloat16)
    target[0, 0:128, 0:128] = t0
    target[0, 0:128, 128:256] = zero
    target[0, 128:256, 0:128] = t1
    target[0, 128:256, 128:256] = t0
    target[1, 0:128, 0:128] = t2
    target[1, 0:128, 128:256] = t1
    target[1, 128:256, 0:128] = zero
    target[1, 128:256, 128:256] = t2


def edge_masks():
    sub = lax.broadcasted_iota(jnp.int32, (8, 128), 0)
    return sub == 0, sub == 7


def shift_down(value, first, fill):
    return jnp.where(first, fill, pltpu.roll(value, 1, 0))


def shift_up(value, last, fill):
    return jnp.where(last, fill, pltpu.roll(value, 7, 0))


def own_pair(pair, plane, part_ref, wide, block, base):
    first, last = edge_masks()
    for x in range(8):
        planes = [plane(2 * pair + half, x) for half in range(2)]
        px = x + 1
        lanes = slice((px % 2) * 128, (px % 2) * 128 + 128)
        for y in range(8):
            mids = [planes[half][y * 8 : y * 8 + 8] for half in range(2)]
            for az, parts in enumerate(
                (
                    [shift_down(mid, first, 0.0) for mid in mids],
                    mids,
                    [shift_up(mid, last, 0.0) for mid in mids],
                )
            ):
                block[az, px // 2, y + 1, :, lanes] = jnp.concatenate(parts, axis=0).astype(jnp.bfloat16)
    acc = jnp.zeros((512, 256), jnp.float32)
    for az in range(3):
        for ay in range(3):
            for side in range(2):
                part = block[az, side : side + 4, ay : ay + 8].reshape(512, 256)
                acc = acc + jnp.dot(part, wide[ay * 3 + az, side], preferred_element_type=jnp.float32)
    if base is None:
        part_ref[pair] = acc
        return
    for half in range(2):
        for x in range(8):
            added = base(2 * pair + half, x)
            lanes = slice((x % 2) * 128, (x % 2) * 128 + 128)
            for y in range(8):
                row = (x // 2) * 128 + y * 16 + half * 8
                part_ref[pair, row : row + 8, lanes] = acc[row : row + 8, lanes] + added[y * 8 : y * 8 + 8]


def own_conv(plane, w_ref, part_ref, wide, block, base=None):
    step = pl.program_id(0)

    @pl.when(step == 0)
    def _():
        block[...] = jnp.zeros_like(block)
        for tap in range(9):
            toeplitz(wide.at[tap], (w_ref[tap], w_ref[9 + tap], w_ref[18 + tap]))

    for pair in range(STEP // 2):
        own_pair(pair, plane, part_ref, wide, block.at[pair], base)


def first_own_kernel(feat_ref, occ_ref, w_ref, part_ref, x_ref, mask_ref, shell_ref, wide, block, cells, inner):
    step = pl.program_id(0)
    rows = lax.broadcasted_iota(jnp.int32, (128, 128), 0)
    cols = lax.broadcasted_iota(jnp.int32, (128, 128), 1)
    diagonal = rows == cols
    ones = jnp.ones((128, 128), jnp.bfloat16)
    held = {}
    for half in range(STEP):
        occupied = occ_ref[pl.ds(step * STEP + half, 1), :].astype(jnp.float32)
        for chunk in range(4):
            at = slice(chunk * 128, chunk * 128 + 128)
            scale = jnp.where(diagonal, jnp.broadcast_to(occupied[:, at], (128, 128)), 0.0).astype(jnp.bfloat16)
            right = jnp.concatenate([feat_ref[half, at, :], ones], axis=1)
            both = jnp.dot(scale, right, preferred_element_type=jnp.float32)
            x_ref[half, at, :] = both[:, :128].astype(jnp.bfloat16)
            mask_ref[half, at, :] = both[:, 128:].astype(jnp.bfloat16)
            held[half, 2 * chunk] = both[:64, :128]
            held[half, 2 * chunk + 1] = both[64:, :128]
        planes = [held[half, x] for x in range(8)]
        store_shell(shell_ref.at[half], planes)
        store_inner(shell_ref.at[half], planes, cells.at[half], inner.at[half])
    own_conv(lambda half, x: held[half, x], w_ref, part_ref, wide, block)


def second_own_kernel(hidden_ref, x_ref, w_ref, part_ref, shell_ref, wide, block, cells, inner):
    plane = lambda ref: lambda half, x: ref[half, x * 64 : x * 64 + 64, :].astype(jnp.float32)
    for half in range(STEP):
        planes = [plane(hidden_ref)(half, x) for x in range(8)]
        store_shell(shell_ref.at[half], planes)
        store_inner(shell_ref.at[half], planes, cells.at[half], inner.at[half])
    own_conv(plane(hidden_ref), w_ref, part_ref, wide, block, plane(x_ref))


def fill_pool(pool, start, source):
    for entry in range(source.shape[0]):
        pool[start + entry] = source[entry].astype(jnp.float32)


def build_face(face, src_ref, pool, halo):
    first, last = edge_masks()
    delta, cell, z_cell = ((0, 7, 7), (2, 0, 0))[face % 2]

    def entry(brick, k):
        ref = src_ref[brick, k]
        return jnp.where(ref < 0, BLANK, ref)

    def put(pair, outer, parts):
        lanes = slice((outer % 2) * 128, (outer % 2) * 128 + 128)
        for shift in range(3):
            both = jnp.concatenate([parts[0][shift], parts[1][shift]], axis=0)
            halo[face, shift, outer // 2, pair * 16 : pair * 16 + 16, lanes] = both.astype(jnp.bfloat16)

    def column(around, x, y):
        below, here, above = around
        start, at_lo, at_hi = ring_row(x, y), cell_row(x, y, 7), cell_row(x, y, 0)
        mid = pool[here, start : start + 8, :]
        lo = jnp.broadcast_to(pool[below, at_lo : at_lo + 1, :], (8, 128))
        hi = jnp.broadcast_to(pool[above, at_hi : at_hi + 1, :], (8, 128))
        return shift_down(mid, first, lo), mid, shift_up(mid, last, hi)

    def z_plane(here, x):
        if x in (0, 7):
            mid = pool[here, pl.ds(ring_row(x, 0) + z_cell, 8, stride=8), :]
        else:
            start = cell_row(x, 1, z_cell) - 1
            at_lo, at_hi = cell_row(x, 0, z_cell), cell_row(x, 7, z_cell)
            mid = pool[here, start : start + 8, :]
            mid = jnp.where(first, jnp.broadcast_to(pool[here, at_lo : at_lo + 1, :], (8, 128)), mid)
            mid = jnp.where(last, jnp.broadcast_to(pool[here, at_hi : at_hi + 1, :], (8, 128)), mid)
        return shift_down(mid, first, 0.0), mid, shift_up(mid, last, 0.0)

    for pair in range(BR // 2):
        bricks = (2 * pair, 2 * pair + 1)
        if face < 2:
            around = [[[entry(b, delta * 9 + dy * 3 + dz) for dz in range(3)] for dy in range(3)] for b in bricks]
            for outer in range(10):
                dy = 0 if outer == 0 else (2 if outer == 9 else 1)
                y = 7 if outer == 0 else (0 if outer == 9 else outer - 1)
                put(pair, outer, [column(around[half][dy], cell, y) for half in range(2)])
        elif face < 4:
            around = [[entry(b, 9 + delta * 3 + dz) for dz in range(3)] for b in bricks]
            for x in range(8):
                put(pair, x + 1, [column(around[half], x, cell) for half in range(2)])
        else:
            here = [entry(b, 12 + delta) for b in bricks]
            for x in range(8):
                put(pair, x + 1, [z_plane(here[half], x) for half in range(2)])


def face_weights(face, w, along):
    end = 2 * (face % 2)
    for shift in range(3):
        taps = (
            [end * 9 + tap * 3 + shift for tap in range(3)],
            [tap * 9 + end * 3 + shift for tap in range(3)],
            [tap * 9 + shift * 3 + end for tap in range(3)],
        )[face // 2]
        toeplitz(along.at[face, shift], [w[tap] for tap in taps])


def sum_face(face, halo, along, sums):
    rows = 8 * BR
    acc = jnp.zeros((4 * rows, 256), jnp.float32)
    for shift in range(3):
        for side in range(2):
            part = halo[face, shift, side : side + 4].reshape(4 * rows, 256)
            acc = acc + jnp.dot(part, along[face, shift, side], preferred_element_type=jnp.float32)
    sums[face] = acc.reshape(4, BR, 8, 256)


def halo_part(odd, src_ref, sources, landed, sems, streams, stream_sems, pool, halo, along, sums):
    loads = start_all([pltpu.make_async_copy(a, b, sems.at[n]) for n, (a, b) in enumerate(zip(sources, landed))])
    pool[BLANK] = jnp.zeros((SHELL, 128), jnp.float32)
    for face in range(2, 6):
        for shift in range(3):
            halo[face, shift, 0, :, 0:128] = jnp.zeros((8 * BR, 128), jnp.bfloat16)
            halo[face, shift, 4, :, 128:256] = jnp.zeros((8 * BR, 128), jnp.bfloat16)
    near, far = BR + EDGE * (1 - odd), BR + EDGE * odd
    for load, start, field in zip(loads[:4], (0, near, far, BR + 2 * EDGE), landed[:4]):
        load.wait()
        if field is landed[3]:
            start_streams(streams, stream_sems)
        fill_pool(pool, start, field)

    build_face(0, src_ref, pool, halo)
    loads[4].wait()
    face_weights(0, landed[4], along)
    for face in range(6):
        if face < 5:
            build_face(face + 1, src_ref, pool, halo)
            face_weights(face + 1, landed[4], along)
        sum_face(face, halo, along, sums)


def start_streams(streams, stream_sems):
    for pair in range(BR // 2):
        for n, (source, target, size) in enumerate(streams):
            at = pl.ds(pair * size, size)
            pltpu.make_async_copy(source.at[at], target.at[at], stream_sems.at[n, pair]).start()


def wait_stream(streams, stream_sems, pair):
    for n, (source, target, size) in enumerate(streams):
        at = pl.ds(pair * size, size)
        pltpu.make_async_copy(source.at[at], target.at[at], stream_sems.at[n, pair]).wait()


def whole_plane(part, sums, pair, half, x):
    first, last = edge_masks()
    brick = pair * 2 + half
    lanes = slice((x % 2) * 128, (x % 2) * 128 + 128)
    columns = []
    for y in range(8):
        row = (x // 2) * 128 + y * 16 + half * 8
        value = part[pair, row : row + 8, lanes]
        if x in (0, 7):
            value = value + sums[x // 7, y // 2, brick, :, (y % 2) * 128 : (y % 2) * 128 + 128]
        if y in (0, 7):
            value = value + sums[2 + y // 7, x // 2, brick, :, lanes]
        lo = jnp.broadcast_to(sums[4, x // 2, brick, y : y + 1, lanes], (8, 128))
        hi = jnp.broadcast_to(sums[5, x // 2, brick, y : y + 1, lanes], (8, 128))
        columns.append(value + jnp.where(first, lo, jnp.where(last, hi, 0.0)))
    return jnp.concatenate(columns, axis=0)


def first_halo_kernel(
    src_ref, send_ref, pick_ref, part_ref, mask_ref, w_ref, shells_ref, near_in_ref, far_in_ref, recv_ref,
    hidden_ref, out_ref, near_ref, far_ref,
    pool, halo, along, sums, w, shells, near, far, recv, part, mask, done, sems, stream_sems, done_sems,
    own, out_sems, cells, inner,
):
    streams = ((part_ref, part, 1), (mask_ref, mask, 2))
    sources = (shells_ref, near_in_ref, far_in_ref, recv_ref, w_ref)
    landed = (shells, near, far, recv, w)
    halo_part(parity(), src_ref, sources, landed, sems, streams, stream_sems, pool, halo, along, sums)

    def store(pair):
        at = pl.ds(pair * 2, 2)
        return pltpu.make_async_copy(done.at[at], hidden_ref.at[at], done_sems.at[pair])

    def pair_body(pair, carry):
        wait_stream(streams, stream_sems, pair)
        for half in range(2):
            brick = pair * 2 + half
            planes = []
            for x in range(8):
                rows = slice(x * 64, x * 64 + 64)
                value = whole_plane(part, sums, pair, half, x)
                value = value * (0.5 + 0.5 * jnp.tanh(0.5 * value)) * mask[brick, rows, :].astype(jnp.float32)
                done[brick, rows, :] = value.astype(jnp.bfloat16)
                planes.append(value)
            store_shell(own.at[brick], planes)
            store_inner(own.at[brick], planes, cells.at[half], inner.at[half])
        store(pair).start()
        return carry

    lax.fori_loop(0, BR // 4, pair_body, 0)
    send_below(send_ref, own, out_ref, out_sems, 0, BR // 2)
    lax.fori_loop(BR // 4, BR // 2, pair_body, 0)
    send_below(send_ref, own, out_ref, out_sems, BR // 2, BR)
    copies = hand_out(send_ref, parity(), own, out_ref, near_ref, far_ref, out_sems, False)
    wait_all([store(pair) for pair in range(BR // 2)])
    wait_all(copies)


def second_halo_kernel(
    src_ref, part_ref, mask_ref, w_ref, shells_ref, near_in_ref, far_in_ref, recv_ref,
    result_ref,
    pool, halo, along, sums, w, shells, near, far, recv, part, mask, done, sems, stream_sems, done_sems,
):
    streams = ((part_ref, part, 1), (mask_ref, mask, 2))
    sources = (shells_ref, near_in_ref, far_in_ref, recv_ref, w_ref)
    landed = (shells, near, far, recv, w)
    halo_part(parity(), src_ref, sources, landed, sems, streams, stream_sems, pool, halo, along, sums)

    def store(pair):
        at = pl.ds(pair * 2, 2)
        return pltpu.make_async_copy(done.at[at], result_ref.at[at], done_sems.at[pair])

    def pair_body(pair, carry):
        wait_stream(streams, stream_sems, pair)
        for half in range(2):
            brick = pair * 2 + half
            for x in range(8):
                rows = slice(x * 64, x * 64 + 64)
                value = whole_plane(part, sums, pair, half, x)
                done[brick, rows, :] = (value * mask[brick, rows, :].astype(jnp.float32)).astype(jnp.bfloat16)
        store(pair).start()
        return carry

    lax.fori_loop(0, BR // 2, pair_body, 0)
    wait_all([store(pair) for pair in range(BR // 2)])


WHOLE = functools.partial(pl.BlockSpec, memory_space=pltpu.VMEM)
SCALARS = functools.partial(pl.BlockSpec, memory_space=pltpu.SMEM)
ANYWHERE = functools.partial(pl.BlockSpec, memory_space=pl.ANY)
STEP = 4
GRID = (BR // STEP,)
FIELD = jax.ShapeDtypeStruct((BR, 512, 128), jnp.bfloat16)
PARTIAL = jax.ShapeDtypeStruct((BR // 2, 512, 256), jnp.float32)


def pair_spec():
    return pl.BlockSpec((STEP, 512, 128), lambda i: (i, 0, 0))


def part_spec():
    return pl.BlockSpec((STEP // 2, 512, 256), lambda i: (i, 0, 0))


def shell_pair_spec():
    return pl.BlockSpec((STEP, SHELL, 128), lambda i: (i, 0, 0))


def shells_of(*counts):
    return [jax.ShapeDtypeStruct((n, SHELL, 128), jnp.bfloat16) for n in counts]


def params():
    return pltpu.CompilerParams(vmem_limit_bytes=VMEM_LIMIT)


def own_scratch():
    return [
        pltpu.VMEM((9, 2, 256, 256), jnp.bfloat16),
        pltpu.VMEM((STEP // 2, 3, 5, 10, 16, 256), jnp.bfloat16),
        pltpu.VMEM((STEP, 512, 128), jnp.float32),
        pltpu.VMEM((STEP, SHELL - FACE_LO, 128), jnp.float32),
    ]


def halo_scratch():
    shells = [pltpu.VMEM((n, SHELL, 128), jnp.bfloat16) for n in (BR, EDGE, EDGE, SLOTS)]
    return [
        pltpu.VMEM((ENTRIES + 1, SHELL, 128), jnp.float32),
        pltpu.VMEM((6, 3, 5, 8 * BR, 256), jnp.bfloat16),
        pltpu.VMEM((6, 3, 2, 256, 256), jnp.bfloat16),
        pltpu.VMEM((6, 4, BR, 8, 256), jnp.float32),
        pltpu.VMEM((27, 128, 128), jnp.bfloat16),
        *shells,
        pltpu.VMEM((BR // 2, 512, 256), jnp.float32),
        pltpu.VMEM((BR, 512, 128), jnp.bfloat16),
        pltpu.VMEM((BR, 512, 128), jnp.bfloat16),
        pltpu.SemaphoreType.DMA((5,)),
        pltpu.SemaphoreType.DMA((2, BR // 2)),
        pltpu.SemaphoreType.DMA((BR // 2,)),
    ]


def own_shells_scratch():
    return [pltpu.VMEM((BR, SHELL, 128), jnp.bfloat16), pltpu.SemaphoreType.DMA((SLOTS + 2,))]


OWN_COST = pl.CostEstimate(flops=2 * 6 * 512 * 4608 * 256, bytes_accessed=8 * MIB, transcendentals=0)
HALO_COST = pl.CostEstimate(flops=2 * 36 * 384 * 256 * 256, bytes_accessed=10 * MIB, transcendentals=0)


def pack(send, feats, occ, pick):
    return pl.pallas_call(
        pack_kernel,
        in_specs=[SCALARS(), ANYWHERE(), WHOLE(), ANYWHERE()],
        out_specs=[ANYWHERE()] * 3,
        out_shape=shells_of(SLOTS, EDGE, EDGE),
        scratch_shapes=[
            pltpu.VMEM((BR, 512, 128), jnp.bfloat16),
            pltpu.VMEM((BR, SHELL, 128), jnp.bfloat16),
            pltpu.VMEM((SHELL, 512), jnp.bfloat16),
            pltpu.SemaphoreType.DMA((BR // 2 + 1,)),
            pltpu.SemaphoreType.DMA((SLOTS + 2,)),
        ],
        compiler_params=params(),
        name="pack_shells",
    )(send, feats, occ, pick)


def first_own(feats, occ, weights):
    return pl.pallas_call(
        first_own_kernel,
        grid=GRID,
        in_specs=[pair_spec(), WHOLE(), WHOLE()],
        out_specs=[part_spec(), pair_spec(), pair_spec(), shell_pair_spec()],
        out_shape=[PARTIAL, FIELD, FIELD] + shells_of(BR),
        scratch_shapes=own_scratch(),
        compiler_params=params(),
        cost_estimate=OWN_COST,
        name="first_own",
    )(feats, occ, weights)


def second_own(hidden, x, weights):
    return pl.pallas_call(
        second_own_kernel,
        grid=GRID,
        in_specs=[pair_spec(), pair_spec(), WHOLE()],
        out_specs=[part_spec(), shell_pair_spec()],
        out_shape=[PARTIAL] + shells_of(BR),
        scratch_shapes=own_scratch(),
        compiler_params=params(),
        cost_estimate=OWN_COST,
        name="second_own",
    )(hidden, x, weights)


def first_halo(src, send, pick, part, mask, weights, shells, near, far, recv):
    return pl.pallas_call(
        first_halo_kernel,
        in_specs=[SCALARS(), SCALARS(), WHOLE()] + [ANYWHERE()] * 7,
        out_specs=[ANYWHERE()] * 4,
        out_shape=[FIELD] + shells_of(SLOTS, EDGE, EDGE),
        scratch_shapes=halo_scratch() + own_shells_scratch() + own_scratch()[2:],
        compiler_params=params(),
        cost_estimate=HALO_COST,
        name="first_halo",
    )(src, send, pick, part, mask, weights, shells, near, far, recv)


def second_halo(src, part, mask, weights, shells, near, far, recv):
    return pl.pallas_call(
        second_halo_kernel,
        in_specs=[SCALARS()] + [ANYWHERE()] * 7,
        out_specs=ANYWHERE(),
        out_shape=FIELD,
        scratch_shapes=halo_scratch(),
        compiler_params=params(),
        cost_estimate=HALO_COST,
        name="second_halo",
    )(src, part, mask, weights, shells, near, far, recv)


def swapped(value, begin):
    axes = ("grp", "dev")
    routes = []
    for device in range(begin, lax.axis_size(axes) - 1, 2):
        routes += [(device, device + 1), (device + 1, device)]
    return lax.ppermute(value, axes, routes)


def exchange(outgoing, near, far):
    arrived = lax.all_to_all(outgoing, "dev", split_axis=0, concat_axis=0, tiled=True)
    return swapped(near, 0), swapped(far, 1), arrived


def per_device(features, occupancy, w_first, w_second, src_ref, send_list):
    send = send_list.reshape(SLOTS)
    pick = shell_matrix()
    outgoing, near, far = pack(send, features, occupancy, pick)
    pick = pick[FACE_LO:]
    around = exchange(outgoing, near, far)
    part, x, mask, shells = first_own(features, occupancy, w_first)
    hidden, outgoing, near, far = first_halo(src_ref, send, pick, part, mask, w_first, shells, *around)
    around = exchange(outgoing, near, far)
    part, shells = second_own(hidden, x, w_second)
    return second_halo(src_ref, part, mask, w_second, shells, *around)


def solution(mesh):
    placed = (
        P(("grp", "dev"), None, None),
        P(("grp", "dev"), None),
        P(),
        P(),
        P(("grp", "dev"), None),
        P(("grp", "dev"), None, None),
    )
    return jax.shard_map(
        per_device,
        mesh=mesh,
        in_specs=placed,
        out_specs=P(("grp", "dev"), None, None),
        check_vma=False,
    )
```
